256 devices in a mesh: shot: 8 (over y, core), gx: 4 (over z_hi), gy: 8 (over z_lo, x).
Axes of the slice: x: 4, y: 4, z: 8 (z_hi: 4, z_lo: 2; z = z_hi * 2 + z_lo), core: 2. Of those that a mesh axis runs over, the one named last changes fastest.
Arguments:
- latent: float32 [32, 24, 4096], P('shot', 'gx', 'gy'), may hold values from -6 to 6
- w_first: float32 [64, 64], replicated, may hold values from -0.75 to 0.75
- w_second: float32 [64, 128], replicated, may hold values from -0.75 to 0.75
- fwd_press: float32 [8, 96, 256, 128], P('shot', 'gx', 'gy'), may hold values from -1.5 to 8
- fwd_vel: float32 [8, 3, 96, 256, 128], P('shot', None, 'gx', 'gy'), may hold values from -1.5 to 8
- adj_press: float32 [8, 96, 256, 128], P('shot', 'gx', 'gy'), may hold values from -1.5 to 8
- adj_vel: float32 [8, 3, 96, 256, 128], P('shot', None, 'gx', 'gy'), may hold values from -1.5 to 8
- src_pos: int32 [3, 8], P(None, 'shot'), may hold values from 0 to 255, as said below
- src_amp: float32 [3, 8], P(None, 'shot'), may hold values from -24 to 24
- rec_pos: int32 [8, 3, 2048], P('shot'), may hold values from 0 to 255, as said below
- observed: float32 [8, 3, 2048], P('shot'), may hold values from -6 to 6
Outputs:
- grad_latent: float32 [32, 24, 4096], P('shot', 'gx', 'gy')
- grad_first: float32 [64, 64], replicated
- grad_second: float32 [64, 128], replicated
The draws below stay inside these ranges and needn't reach their ends.
Inputs may be any that keep to these rules, and one draw needn't show every extreme that they name: `src_pos`: row 0 is an x cell below 96, row 1 a y cell below 256, row 2 a depth cell below 128. `rec_pos`: component 0 is an x cell below 96, component 1 a y cell below 256, component 2 a depth cell below 128; cells may repeat.
All inputs are finite; a program needn't handle non-finite values.
Results may differ from the reference program's by a relative error of at most 0.0003.
Values sent between devices are 32-bit elements; how exact they have to be, the bound alone decides.
No kernel may reach another device: no remote copies, remote signals or barrier semaphores. Data moves between devices by JAX's collectives and lax.ppermute only.
A program may use at most 64 MiB of HBM per device.

```python
import jax
import jax.numpy as jnp
from jax import lax

NZ = 128
NREC = 2048
CH = 64
STEPS = 3
OUTS = 128
NX = 96
NY = 256
SHOTS = 8
XC = 24
YC = 64
ZC = 32


def draw_src_pos(key, part):
    subkeys = jax.random.split(jax.random.fold_in(key, 11), 3)
    along_x = jax.random.randint(subkeys[0], (SHOTS,), 0, NX).at[0].set(NX - 1).at[1].set(0)
    along_y = jax.random.randint(subkeys[1], (SHOTS,), 0, NY).at[0].set(NY - 1)
    along_z = jax.random.randint(subkeys[2], (SHOTS,), 0, NZ).at[0].set(NZ - 1)
    return jnp.stack([along_x, along_y, along_z]).astype(jnp.int32)


def draw_rec_pos(key, part):
    subkeys = jax.random.split(jax.random.fold_in(key, 23), 3)
    along_x = jax.random.randint(subkeys[0], (SHOTS, NREC), 0, NX).at[:, 0].set(NX - 1).at[:, 1].set(0)
    along_y = jax.random.randint(subkeys[1], (SHOTS, NREC), 0, NY).at[:, 0].set(NY - 1)
    along_z = jax.random.randint(subkeys[2], (SHOTS, NREC), 0, NZ).at[:, 0].set(NZ - 1)
    return jnp.stack([along_x, along_y, along_z], axis=1).astype(jnp.int32)


def smooth_along(values_in, axis_id, spread):
    length = values_in.shape[axis_id]
    places = jnp.arange(length, dtype=jnp.float32)
    kernel = jnp.exp(-0.5 * jnp.square((places[:, None] - places[None, :]) / spread))
    kernel = kernel / jnp.sum(kernel, axis=1, keepdims=True)
    rotated = jnp.moveaxis(values_in, axis_id, -1)
    return jnp.moveaxis(jnp.dot(rotated, kernel.T), -1, axis_id)


def taper(length):
    places = jnp.arange(length, dtype=jnp.float32)
    distance = jnp.minimum(places, length - 1.0 - places)
    return jnp.square(jnp.sin(0.5 * jnp.pi * jnp.minimum(1.0, (distance + 0.5) / 6.0)))


def wavefield(key, leading):
    subkeys = jax.random.split(key, 2)
    full_shape = leading + (NX, NY, NZ)
    dimensions = len(full_shape)
    white_noise = jax.random.normal(subkeys[0], full_shape, jnp.float32)
    spread = 3.0
    smooth = white_noise
    for axis_id in (dimensions - 3, dimensions - 2, dimensions - 1):
        smooth = smooth_along(smooth, axis_id, spread)
    smooth = smooth / jnp.sqrt(jnp.mean(jnp.square(smooth)) + 1e-12)
    smooth = jnp.clip(smooth, -3.0, 3.0)
    envelope = taper(NX)[:, None, None] * taper(NY)[None, :, None] * taper(NZ)[None, None, :]
    rough_part = 0.12 * jax.random.normal(subkeys[1], full_shape, jnp.float32)
    wave_field = envelope * (2.5 + smooth) + rough_part
    return jnp.clip(wave_field, -1.5, 8.0).astype(jnp.float32)


def draw_fwd_press(key, part):
    return wavefield(jax.random.fold_in(key, 31), (SHOTS,))


def draw_fwd_vel(key, part):
    return wavefield(jax.random.fold_in(key, 37), (SHOTS, 3))


def draw_adj_press(key, part):
    return wavefield(jax.random.fold_in(key, 41), (SHOTS,))


def draw_adj_vel(key, part):
    return wavefield(jax.random.fold_in(key, 43), (SHOTS, 3))


def shard_levels(key, dims, cuts, smallest, high):
    def one(position, blocks):
        steps = jax.random.uniform(jax.random.fold_in(jax.random.fold_in(key, 6), position), (blocks,), jnp.float32, smallest / len(cuts), high / len(cuts))
        return jnp.repeat(jnp.exp(steps), dims[position] // blocks).reshape((-1,) + (1,) * (len(dims) - position - 1))

    loudness = one(*cuts[0])
    for cut in cuts[1:]:
        loudness = loudness * one(*cut)
    return loudness


def scatter_about(key, extent, width, reach, cuts=(), kind=jnp.bfloat16):
    level = shard_levels(key, extent, cuts, -0.22, 0.18) if cuts else 1.0
    result = jax.random.normal(key, extent, jnp.float32) * width * level
    return jnp.minimum(jnp.maximum(result, -reach), reach).astype(kind)


def setup_inputs(seed: int = 0) -> dict:
    streams_of = jax.random.split(jax.random.key(seed), 12)
    latent = scatter_about(streams_of[0], (ZC, XC, YC * CH), 1.0, 6.0, ((0, 8), (1, 4), (2, 8)), jnp.float32)
    w_first = scatter_about(streams_of[1], (CH, CH), CH ** -0.5, 0.75, (), jnp.float32)
    w_second = scatter_about(streams_of[2], (CH, OUTS), CH ** -0.5, 0.75, (), jnp.float32)
    fwd_press = draw_fwd_press(jax.random.fold_in(streams_of[11], 71), 0)
    fwd_vel = draw_fwd_vel(jax.random.fold_in(streams_of[11], 71), 0)
    adj_press = draw_adj_press(jax.random.fold_in(streams_of[11], 71), 0)
    adj_vel = draw_adj_vel(jax.random.fold_in(streams_of[11], 71), 0)
    src_pos = draw_src_pos(jax.random.fold_in(streams_of[11], 71), 0)
    src_amp = scatter_about(streams_of[8], (STEPS, SHOTS), 4.0, 24.0, ((1, 8),), jnp.float32)
    rec_pos = draw_rec_pos(jax.random.fold_in(streams_of[11], 71), 0)
    observed = scatter_about(streams_of[10], (SHOTS, STEPS, NREC), 1.0, 6.0, ((0, 8),), jnp.float32)
    return dict(latent=latent, w_first=w_first, w_second=w_second, fwd_press=fwd_press, fwd_vel=fwd_vel, adj_press=adj_press, adj_vel=adj_vel, src_pos=src_pos, src_amp=src_amp, rec_pos=rec_pos, observed=observed)


coeffs = (1225.0 / 1024.0, -245.0 / 3072.0, 49.0 / 5120.0, -5.0 / 7168.0)


def take_slab(values_in, axis_id, start_at, length):
    return lax.slice_in_dim(values_in, start_at, start_at + length, axis=axis_id)


def diff_plus(extended, axis_id, start_at, length):
    summed = 0.0
    for order, weight in enumerate(coeffs):
        offset = order + 1
        summed = summed + weight * (take_slab(extended, axis_id, start_at + offset, length) - take_slab(extended, axis_id, start_at - offset + 1, length))
    return summed


def diff_minus(extended, axis_id, start_at, length):
    summed = 0.0
    for order, weight in enumerate(coeffs):
        offset = order + 1
        summed = summed + weight * (take_slab(extended, axis_id, start_at + offset - 1, length) - take_slab(extended, axis_id, start_at - offset, length))
    return summed


def edge_pad(field_in, axis_id):
    widths = [(0, 0), (0, 0), (0, 0)]
    widths[axis_id] = (4, 4)
    return jnp.pad(field_in, widths)


def wave_step(pressure, vel_x, vel_y, vel_z, modulus, buoyancy):
    size_x, size_y, size_z = pressure.shape
    grad_x = diff_plus(edge_pad(pressure, 0), 0, 4, size_x)
    grad_y = diff_plus(edge_pad(pressure, 1), 1, 4, size_y)
    grad_z = diff_plus(edge_pad(pressure, 2), 2, 4, size_z)
    vel_x = vel_x - buoyancy * grad_x
    vel_y = vel_y - buoyancy * grad_y
    vel_z = vel_z - buoyancy * grad_z
    diverge = diff_minus(edge_pad(vel_x, 0), 0, 4, size_x) + diff_minus(edge_pad(vel_y, 1), 1, 4, size_y) + diff_minus(edge_pad(vel_z, 2), 2, 4, size_z)
    pressure = pressure - modulus * diverge
    return pressure, vel_x, vel_y, vel_z, diverge, grad_x, grad_y, grad_z


def decode(latent, w_first, w_second):
    depth_c, rows_x, merged = latent.shape
    rows_y = merged // CH
    flattened = latent.reshape(-1, CH)
    hidden = jnp.tanh(jnp.dot(flattened, w_first, precision=lax.Precision.HIGHEST))
    outputs = jnp.dot(hidden, w_second, precision=lax.Precision.HIGHEST)
    fine_out = outputs.reshape(depth_c, rows_x, rows_y, 2, 4, 4, 4).transpose(3, 1, 4, 2, 5, 0, 6).reshape(2, rows_x * 4, rows_y * 4, depth_c * 4)
    return flattened, hidden, fine_out


def materials(fine_out):
    wave_speed = 0.15 + 0.25 * jax.nn.sigmoid(fine_out[0])
    density = 1.0 + 1.5 * jax.nn.sigmoid(fine_out[1])
    return density * wave_speed * wave_speed, 1.0 / density


def decoder_grads(flattened, hidden, fine_out, grad_mod, grad_buoy, w_first, w_second):
    sig_speed = jax.nn.sigmoid(fine_out[0])
    sig_dens = jax.nn.sigmoid(fine_out[1])
    wave_speed = 0.15 + 0.25 * sig_speed
    density = 1.0 + 1.5 * sig_dens
    grad_speed = grad_mod * 2.0 * density * wave_speed
    grad_dens = grad_mod * wave_speed * wave_speed - grad_buoy / (density * density)
    grad_fine = jnp.stack([grad_speed * 0.25 * sig_speed * (1.0 - sig_speed), grad_dens * 1.5 * sig_dens * (1.0 - sig_dens)])
    size_x, size_y, size_z = grad_fine.shape[1], grad_fine.shape[2], grad_fine.shape[3]
    grad_out = grad_fine.reshape(2, size_x // 4, 4, size_y // 4, 4, size_z // 4, 4).transpose(5, 1, 3, 0, 2, 4, 6).reshape(-1, 128)
    grad_hidden = jnp.dot(grad_out, w_second.T, precision=lax.Precision.HIGHEST)
    grad_pre = grad_hidden * (1.0 - hidden * hidden)
    grad_latent = jnp.dot(grad_pre, w_first.T, precision=lax.Precision.HIGHEST).reshape(size_z // 4, size_x // 4, (size_y // 4) * CH)
    grad_second = jnp.dot(hidden.T, grad_out, precision=lax.Precision.HIGHEST)
    grad_first = jnp.dot(flattened.T, grad_pre, precision=lax.Precision.HIGHEST)
    return grad_latent, grad_first, grad_second


def reference(latent, w_first, w_second, fwd_press, fwd_vel, adj_press, adj_vel, src_pos, src_amp, rec_pos, observed):
    flattened, hidden, fine_out = decode(latent, w_first, w_second)
    modulus, buoyancy = materials(fine_out)

    def one_shot(totals, inputs):
        grad_mod, grad_buoy = totals
        start_press, start_vel, back_press, back_vel, source, amplitudes, receivers, observed_now = inputs
        pressure, vel_x, vel_y, vel_z = start_press, start_vel[0], start_vel[1], start_vel[2]
        stored = []
        misfits = []
        for moment in range(STEPS):
            pressure, vel_x, vel_y, vel_z, diverge, grad_x, grad_y, grad_z = wave_step(pressure, vel_x, vel_y, vel_z, modulus, buoyancy)
            pressure = pressure.at[source[0], source[1], source[2]].add(amplitudes[moment])
            misfits.append(pressure[receivers[0], receivers[1], receivers[2]] - observed_now[moment])
            stored.append((diverge, grad_x, grad_y, grad_z))
        pressure, vel_x, vel_y, vel_z = back_press, back_vel[0], back_vel[1], back_vel[2]
        for moment in reversed(range(STEPS)):
            pressure = pressure.at[receivers[0], receivers[1], receivers[2]].add(misfits[moment])
            pressure, vel_x, vel_y, vel_z, diverge, grad_x, grad_y, grad_z = wave_step(pressure, vel_x, vel_y, vel_z, modulus, buoyancy)
            grad_mod = grad_mod - pressure * stored[moment][0]
            grad_buoy = grad_buoy - (vel_x * stored[moment][1] + vel_y * stored[moment][2] + vel_z * stored[moment][3])
        return (grad_mod, grad_buoy), None

    zeros = jnp.zeros(modulus.shape, jnp.float32)
    totals, _ignored = lax.scan(one_shot, (zeros, zeros), (fwd_press, fwd_vel, adj_press, adj_vel, src_pos.T, src_amp.T, rec_pos, observed))
    grad_latent, grad_first, grad_second = decoder_grads(flattened, hidden, fine_out, totals[0], totals[1], w_first, w_second)
    return grad_latent, grad_first, grad_second
```

```python
import functools

import jax
import jax.numpy as jnp
from jax import lax
from jax.experimental import pallas as pl
from jax.experimental.pallas import tpu as pltpu
from jax.sharding import PartitionSpec as P

CH = 64
STEPS = 3
coeffs = (1225.0 / 1024.0, -245.0 / 3072.0, 49.0 / 5120.0, -5.0 / 7168.0)

NXT, NYT, NZ = 24, 32, 128
GROUPS = 12
HP = 7
HV = 4
HI = lax.Precision.HIGHEST
F32 = jnp.float32
VMEM = pl.BlockSpec(memory_space=pltpu.VMEM)
SMEM = pl.BlockSpec(memory_space=pltpu.SMEM)


def shape(*dims):
    return jax.ShapeDtypeStruct(dims, F32)


def call(kernel, outs, smem_count, args, scratch=(), flops=10**7):
    nbytes = 4 * sum(a.size for a in args) + 4 * sum(o.size for o in outs)
    return pl.pallas_call(
        kernel,
        out_shape=tuple(outs),
        in_specs=[SMEM] * smem_count + [VMEM] * (len(args) - smem_count),
        out_specs=tuple(VMEM for _ in outs),
        scratch_shapes=list(scratch),
        compiler_params=pltpu.CompilerParams(vmem_limit_bytes=24 * 1024 * 1024),
        cost_estimate=pl.CostEstimate(flops=flops, bytes_accessed=nbytes, transcendentals=0),
    )(*args)


def ring(value, axis, shift):
    count = lax.axis_size(axis)
    return lax.ppermute(value, axis, [(i, (i + shift) % count) for i in range(count)])


def up_rows(value, shift):
    rows = value.shape[0]
    return value if shift == 0 else pltpu.roll(value, (-shift) % rows, 0)


def up_depth(value, shift, lane):
    if shift == 0:
        return value
    rolled = pltpu.roll(value, (-shift) % NZ, 1)
    keep = lane < NZ - shift if shift > 0 else lane >= -shift
    return jnp.where(keep, rolled, 0.0)


def plus(take):
    summed = coeffs[0] * (take(1) - take(0))
    for r in (2, 3, 4):
        summed = summed + coeffs[r - 1] * (take(r) - take(1 - r))
    return summed


def minus(take):
    summed = coeffs[0] * (take(0) - take(-1))
    for r in (2, 3, 4):
        summed = summed + coeffs[r - 1] * (take(r - 1) - take(-r))
    return summed


def step_kernel(moment, forward, last, off_p, off_v, row_p, row_v, *refs):
    refs = list(refs)
    take = refs.pop
    ints = take(0)
    amps = take(0) if forward else None
    press, pxl, pxh, pyl, pyh = [take(0) for _ in range(5)]
    vel, vxl, vxh, vyl, vyh = [take(0) for _ in range(5)]
    buoy, bxl, bxh, byl, byh, modu = [take(0) for _ in range(6)]
    if forward:
        count, obs = take(0), take(0)
        back = take(0) if last else None
    else:
        div_in, slope_in = take(0), take(0)
        gm_in, gb_in = (None, None) if moment == STEPS - 1 else (take(0), take(0))
        inject = None if last else take(0)
    if forward:
        div_out, slope_out = take(0), take(0)
        inject_out = None if last else take(0)
    else:
        gm_out, gb_out = take(0), take(0)
    ends = forward or not last
    if ends:
        p_out, sxl, sxh, syl, syh = [take(0) for _ in range(5)]
    if not last:
        vel_out, vxl_out, vxh_out, vyl_out, vyh_out = [take(0) for _ in range(5)]
    wide, vx = take(0), take(0)

    low_x = ints[0].astype(F32)
    high_x = ints[1].astype(F32)
    low_y = ints[2].astype(F32)
    high_y = ints[3].astype(F32)
    for i in range(HP):
        wide[i] = pxl[off_p + i] * low_x
        wide[HP + NXT + i] = pxh[off_p + i] * high_x

    def copy(x, carry):
        wide[x + HP] = press[x]
        return carry

    lax.fori_loop(0, NXT, copy, 0, unroll=4)

    def slope_x(i):
        return plus(lambda s: wide[i + 3 + s])

    for i in range(HV):
        vx[i] = low_x * (vxl[off_v + i] - bxl[i] * slope_x(i))
        if not last:
            vxl_out[i] = vx[i]
    for i in range(HV - 1):
        at = HV + NXT + i
        vx[at] = high_x * (vxh[off_v + i] - bxh[i] * slope_x(at))
        if not last:
            vxh_out[i] = vx[at]
    if not last:
        vxh_out[HV - 1] = jnp.zeros((NYT, NZ), F32)

    def first(x, carry):
        slope = slope_x(x + HV)
        new = vel[0, x] - buoy[x] * slope
        vx[x + HV] = new
        if not last:
            vel_out[0, x] = new
        if forward:
            slope_out[0, x] = slope
        return carry

    lax.fori_loop(0, NXT, first, 0, unroll=2)

    lane = lax.broadcasted_iota(jnp.int32, (NYT, NZ), 1)
    if forward:
        cell = lax.broadcasted_iota(jnp.int32, (NYT, NZ), 0) * NZ + lane
        source_x = ints[4]
        source_at = ints[5] * NZ + ints[6]
        amplitude = amps[moment, 0]

    def second(x, carry):
        here = wide[x + HP]
        b_here = buoy[x]
        tall = jnp.concatenate(
            [pyl[x, row_p : row_p + 8] * low_y, here, pyh[x, row_p : row_p + 8] * high_y], axis=0
        )
        slope_y = plus(lambda s: up_rows(tall, s))
        vy_low = low_y * (vyl[x, row_v : row_v + 8] - byl[x] * slope_y[0:8])
        vy = vel[1, x] - b_here * slope_y[8:40]
        vy_high = high_y * (vyh[x, row_v : row_v + 8] - byh[x] * slope_y[40:48])
        slope_z = plus(lambda s: up_depth(here, s, lane))
        vz = vel[2, x] - b_here * slope_z
        vy_tall = jnp.concatenate([vy_low, vy, vy_high], axis=0)
        diverge = minus(lambda s: vx[x + HV + s])
        diverge = diverge + minus(lambda s: up_rows(vy_tall, s))[8:40]
        diverge = diverge + minus(lambda s: up_depth(vz, s, lane))
        new = here - modu[x] * diverge
        if forward:
            div_out[x] = diverge
            slope_out[1, x] = slope_y[8:40]
            slope_out[2, x] = slope_z
            at = jnp.where(x == source_x, source_at, -1)
            new = new + jnp.where(cell == at, amplitude, 0.0)
            misfit = count[x] * new - obs[moment, x]
            if last:
                new = back[x] + misfit
            else:
                inject_out[x] = misfit
        else:
            part_m = new * div_in[x]
            part_b = vx[x + HV] * slope_in[0, x] + vy * slope_in[1, x] + vz * slope_in[2, x]
            if gm_in is None:
                gm_out[x] = -part_m
                gb_out[x] = -part_b
            else:
                gm_out[x] = gm_in[x] - part_m
                gb_out[x] = gb_in[x] - part_b
            if not last:
                new = new + inject[x]
        if ends:
            p_out[x] = new
            syl[x] = new[0:8]
            syh[x] = new[24:32]
        if not last:
            vel_out[1, x] = vy
            vel_out[2, x] = vz
            vyl_out[x] = vy_low
            vyh_out[x] = vy_high
        return carry

    lax.fori_loop(0, NXT, second, 0, unroll=2)
    if ends:
        for i in range(HP):
            sxl[i] = p_out[i]
            sxh[i] = p_out[NXT - HP + i]


def step(moment, forward, last, offsets, ints, amps, press, vel, material, extra):
    tile = shape(NXT, NYT, NZ)
    three = shape(3, NXT, NYT, NZ)
    beside_y = shape(NXT, 8, NZ)
    outs = [tile, three if forward else tile]
    if forward and not last:
        outs.append(tile)
    if forward or not last:
        outs += [tile, shape(HP, NYT, NZ), shape(HP, NYT, NZ), beside_y, beside_y]
    if not last:
        outs += [three, shape(HV, NYT, NZ), shape(HV, NYT, NZ), beside_y, beside_y]
    scalars = [ints, amps] if forward else [ints]
    args = scalars + list(press) + list(vel) + list(material) + list(extra)
    scratch = [pltpu.VMEM((NXT + 2 * HP, NYT, NZ), F32), pltpu.VMEM((NXT + 2 * HV, NYT, NZ), F32)]
    kernel = functools.partial(step_kernel, moment, forward, last, *offsets)
    return call(kernel, outs, len(scalars), args, scratch)


def exchange(low_x, high_x, low_y, high_y):
    return (
        ring(high_x, "gx", 1),
        ring(low_x, "gx", -1),
        ring(high_y, "gy", 1),
        ring(low_y, "gy", -1),
    )


def spread_rows(me, sign):
    row = lax.broadcasted_iota(jnp.int32, (32, NZ), 0)
    lane = lax.broadcasted_iota(jnp.int32, (32, NZ), 1)
    owner = (me + sign * (row >> 2)) & 7
    return jnp.where((lane >> 2) == owner * 4 + (row & 3), 1.0, 0.0).astype(F32)


def dot(a, b, dims=((1,), (0,))):
    return lax.dot_general(a, b, (dims, ((), ())), precision=HI, preferred_element_type=F32)


def decode_kernel(ints, mix_first, mix_second, *refs):
    blocks, refs = refs[:8], refs[8:]
    modu, buoy, bxl, bxh, byl, byh, sig_speed, sig_dens, latent_out, hidden_out, rows = refs
    for d in range(8):
        rows[4 * d : 4 * d + 4, :] = blocks[d][...]
    spread = spread_rows(ints[8], -1)
    phase = lax.broadcasted_iota(jnp.int32, (128, NZ), 1) & 3
    for g in range(GROUPS):
        a, half = divmod(g, 2)
        latent = dot(rows[:, 256 * g : 256 * g + 256], spread, ((0,), (0,)))
        hidden = jnp.tanh(dot(mix_first[...], latent))
        latent_out[g] = latent
        hidden_out[g] = hidden
        out = dot(mix_second[...], hidden)
        fine = out[0:128]
        for k in (1, 2, 3):
            fine = jnp.where(phase == k, out[128 * k : 128 * k + 128], fine)
        sig = jax.nn.sigmoid(fine)
        speed = 0.15 + 0.25 * sig[0:64]
        dens = 1.0 + 1.5 * sig[64:128]
        mod = dens * speed * speed
        inv = 1.0 / dens
        for i in range(4):
            x = 4 * a + i
            ys = slice(16 * half, 16 * half + 16)
            part = slice(16 * i, 16 * i + 16)
            sig_speed[x, ys] = sig[0:64][part]
            sig_dens[x, ys] = sig[64:128][part]
            modu[x, ys] = mod[part]
            buoy[x, ys] = inv[part]
    for i in range(HV):
        bxl[i] = buoy[i]
        bxh[i] = buoy[NXT - HV + i]
    byl[...] = buoy[:, 0:8, :]
    byh[...] = buoy[:, 24:32, :]


def grads_kernel(
    ints, mix_first, mix_second, order, gm, gb, sig_speed, sig_dens, latent_in, hidden_in, *refs
):
    sends, refs = refs[:8], refs[8:]
    second_sum, first_sum, chunks = refs
    me = ints[8]
    spread = spread_rows(me, 1)
    phase = lax.broadcasted_iota(jnp.int32, (128, NZ), 1) & 3
    for g in range(GROUPS):
        a, half = divmod(g, 2)
        parts_speed, parts_dens = [], []
        for i in range(4):
            x = 4 * a + i
            ys = slice(16 * half, 16 * half + 16)
            s1, s2 = sig_speed[x, ys], sig_dens[x, ys]
            g_mod, g_buoy = gm[x, ys], gb[x, ys]
            speed = 0.15 + 0.25 * s1
            dens = 1.0 + 1.5 * s2
            grad_speed = g_mod * 2.0 * dens * speed
            grad_dens = g_mod * speed * speed - g_buoy / (dens * dens)
            parts_speed.append(grad_speed * 0.25 * s1 * (1.0 - s1))
            parts_dens.append(grad_dens * 1.5 * s2 * (1.0 - s2))
        fine = jnp.concatenate(parts_speed + parts_dens, axis=0)
        by_phase = jnp.concatenate([jnp.where(phase == k, fine, 0.0) for k in range(4)], axis=0)
        latent, hidden = latent_in[g], hidden_in[g]
        grad_hidden = dot(mix_second[...], by_phase, ((0,), (0,)))
        grad_pre = grad_hidden * (1.0 - hidden * hidden)
        grad_latent = dot(mix_first[...], grad_pre, ((0,), (0,)))
        gathered = dot(spread, grad_latent, ((1,), (1,)))
        for d in range(8):
            for t in range(2):
                row = 8 * g + 4 * t
                sends[d][row : row + 4, :] = gathered[4 * d : 4 * d + 4, 128 * t : 128 * t + 128]
        second = dot(hidden, by_phase, ((1,), (1,)))
        first = dot(latent, grad_pre, ((1,), (1,)))
        if g == 0:
            second_sum[...] = second
            first_sum[...] = first
        else:
            second_sum[...] += second
            first_sum[...] += first
    column = lax.broadcasted_iota(jnp.int32, (CH, 512), 1)
    total = jnp.zeros((CH, 512), F32)
    for b in range(4):
        rows = second_sum[64 * b : 64 * b + 64, :]
        total = total + jnp.where(((column >> 2) & 3) == b, rows, 0.0)
    total = dot(total, order[...])
    corner = first_sum[0:64, 0:64]
    for b in (1, 2, 3):
        corner = corner + first_sum[64 * b : 64 * b + 64, 64 * b : 64 * b + 64]
    packed = jnp.concatenate(
        [total, jnp.concatenate([corner[0:32], corner[32:64]], axis=1)], axis=0
    )
    for j in range(8):
        chunks[j] = packed[12 * j : 12 * j + 12]
    for d in range(8):
        sends[d][96:108, :] = chunks[(me + d) & 7]


def sum_kernel(*refs):
    parts, latent_out, weights_out = refs[:8], refs[8], refs[9]
    total = parts[0][...]
    for part in parts[1:]:
        total = total + part[...]
    for q in range(24):
        a, t = divmod(q, 4)
        for c in range(4):
            latent_out[c, a : a + 1, 128 * t : 128 * t + 128] = total[4 * q + c : 4 * q + c + 1]
    weights_out[...] = total[96:108]


def receiver_fields(rec_pos, observed, anchor_x, anchor_y):
    local_x = rec_pos[0] - anchor_x
    local_y = rec_pos[1] - anchor_y
    inside = (local_x >= 0) & (local_x < NXT) & (local_y >= 0) & (local_y < NYT)
    row = jnp.where(inside, local_x * NYT + local_y, -1)
    rows = (lax.broadcasted_iota(jnp.int32, (NXT * NYT, row.shape[0]), 0) == row).astype(
        jnp.bfloat16
    )
    coarse = lax.reduce_precision(observed, 8, 7)
    rest = observed - coarse
    values = jnp.concatenate([jnp.ones((1, row.shape[0]), F32), coarse, rest], axis=0)
    hit = lax.broadcasted_iota(jnp.int32, (row.shape[0], NZ), 1) == rec_pos[2][:, None]
    spread = jnp.where(hit[:, None, :], values.T[:, :, None], 0.0).astype(jnp.bfloat16)
    fields = jnp.dot(
        rows, spread.reshape(row.shape[0], 7 * NZ), preferred_element_type=F32
    ).reshape(NXT, NYT, 7, NZ)
    fields = fields.transpose(2, 0, 1, 3)
    return fields[0], fields[1:4] + fields[4:7]


def body(
    latent,
    w_first,
    w_second,
    fwd_press,
    fwd_vel,
    adj_press,
    adj_vel,
    src_pos,
    src_amp,
    rec_pos,
    observed,
):
    shot, at_x, at_y = (lax.axis_index(axis) for axis in ("shot", "gx", "gy"))
    anchor_x, anchor_y = at_x * NXT, at_y * NYT
    source_x, source_y = src_pos[0, 0] - anchor_x, src_pos[1, 0] - anchor_y
    inside = (source_x >= 0) & (source_x < NXT) & (source_y >= 0) & (source_y < NYT)
    ints = jnp.stack(
        [
            at_x > 0,
            at_x < lax.axis_size("gx") - 1,
            at_y > 0,
            at_y < lax.axis_size("gy") - 1,
            jnp.where(inside, source_x, -1),
            source_y,
            src_pos[2, 0],
            inside,
            shot,
        ]
    ).astype(jnp.int32)

    flat = latent.reshape(4, 6 * 512)
    blocks = [flat] + [ring(flat, "shot", d) for d in range(1, 8)]

    press, back_press = fwd_press[0], adj_press[0]
    vel, back_vel = fwd_vel[0], adj_vel[0]
    beside = exchange(
        jnp.concatenate([press[:HP], vel[0, :HV], back_vel[0, :HV]], axis=0),
        jnp.concatenate([press[-HP:], vel[0, -HV:], back_vel[0, -HV:]], axis=0),
        jnp.concatenate([press[:, :8], vel[1, :, :8], back_vel[1, :, :8]], axis=1),
        jnp.concatenate([press[:, -8:], vel[1, :, -8:], back_vel[1, :, -8:]], axis=1),
    )
    count, obs = receiver_fields(rec_pos[0], observed[0], anchor_x, anchor_y)

    same = jnp.eye(4, dtype=F32)
    mix_first = (same[:, None, :, None] * w_first.T[None, :, None, :]).reshape(256, 256)
    by_phase = w_second.reshape(CH, 2, 4, 4, 4).transpose(4, 1, 2, 3, 0)
    mix_second = (
        by_phase[:, :, :, None, :, None, :] * same[None, None, None, :, None, :, None]
    ).reshape(512, 256)
    column = lax.broadcasted_iota(jnp.int32, (512, 128), 0)
    natural = (((column >> 4) & 7) << 4) + ((column & 3) << 2) + (column >> 7)
    order = (natural == lax.broadcasted_iota(jnp.int32, (512, 128), 1)).astype(F32)

    tile = shape(NXT, NYT, NZ)
    beside_x, beside_y = shape(HV, NYT, NZ), shape(NXT, 8, NZ)
    decoded = call(
        decode_kernel,
        [tile, tile, beside_x, beside_x, beside_y, beside_y, tile, tile]
        + [shape(GROUPS, 256, NZ)] * 2,
        1,
        [ints, mix_first, mix_second] + blocks,
        [pltpu.VMEM((32, 6 * 512), F32)],
    )
    modulus, buoyancy = decoded[:2]
    material = (buoyancy,) + exchange(*decoded[2:6]) + (modulus,)
    sig_speed, sig_dens, latent_wide, hidden_wide = decoded[6:]

    stored, injects = [], []
    state_p = (press,) + beside
    state_v = (vel,) + beside
    offsets = (0, HP, 0, 8)
    for moment in range(STEPS):
        last = moment == STEPS - 1
        extra = [count, obs] + ([back_press] if last else [])
        outs = step(
            moment, True, last, offsets, ints, src_amp, state_p, state_v, material, extra
        )
        stored.append(outs[:2])
        outs = outs[2:]
        if not last:
            injects.append(outs[0])
            outs = outs[1:]
            state_v = outs[5:]
        state_p = (outs[0],) + exchange(*outs[1:5])
        offsets = (0, 0, 0, 0)
    state_v = (back_vel,) + beside
    offsets = (0, HP + HV, 0, 16)
    sums = []
    for moment in reversed(range(STEPS)):
        last = moment == 0
        extra = list(stored[moment]) + sums + ([] if last else [injects[moment - 1]])
        outs = step(moment, False, last, offsets, ints, None, state_p, state_v, material, extra)
        sums = list(outs[:2])
        if not last:
            state_p = (outs[2],) + exchange(*outs[3:7])
            state_v = outs[7:]
        offsets = (0, 0, 0, 0)

    sends = call(
        grads_kernel,
        [shape(108, 128)] * 8,
        1,
        [ints, mix_first, mix_second, order] + sums + [sig_speed, sig_dens]
        + [latent_wide, hidden_wide],
        [pltpu.VMEM((256, 512), F32), pltpu.VMEM((256, 256), F32), pltpu.VMEM((8, 12, 128), F32)],
    )
    parts = [sends[0]] + [ring(sends[d], "shot", d) for d in range(1, 8)]
    grad_latent, weights = call(sum_kernel, [shape(4, 6, 512), shape(12, 128)], 0, parts)
    group = lax.axis_size("gx") * lax.axis_size("gy")
    weights = lax.all_to_all(
        jnp.broadcast_to(weights, (group, 12, 128)), ("gx", "gy"), 0, 0, tiled=True
    )
    weights = jnp.sum(weights, axis=0)
    weights = lax.all_to_all(jnp.broadcast_to(weights, (8, 12, 128)), "shot", 0, 0, tiled=True)
    weights = weights.reshape(96, 128)
    grad_second = weights[:64]
    grad_first = jnp.concatenate([weights[64:, :64], weights[64:, 64:]], axis=0)
    return (grad_latent, grad_first, grad_second)


def solution(mesh):
    in_specs = (
        P("shot", "gx", "gy"),
        P(),
        P(),
        P("shot", "gx", "gy", None),
        P("shot", None, "gx", "gy", None),
        P("shot", "gx", "gy", None),
        P("shot", None, "gx", "gy", None),
        P(None, "shot"),
        P(None, "shot"),
        P("shot", None, None),
        P("shot", None, None),
    )
    out_specs = (P("shot", "gx", "gy"), P(), P())
    return jax.shard_map(body, mesh=mesh, in_specs=in_specs, out_specs=out_specs, check_vma=False)
```

```python
import functools

import jax
import jax.numpy as jnp
from jax import lax
from jax.experimental import pallas as pl
from jax.experimental.pallas import tpu as pltpu
from jax.sharding import PartitionSpec as P

CH = 64
STEPS = 3
coeffs = (1225.0 / 1024.0, -245.0 / 3072.0, 49.0 / 5120.0, -5.0 / 7168.0)

NXT, NYT, NZ = 24, 32, 128
GROUPS = 12
HP = 7
HV = 4
HI = lax.Precision.HIGHEST
F32 = jnp.float32
BF16 = jnp.bfloat16
UNROLL = (8, 8, 8)
VMEM = pl.BlockSpec(memory_space=pltpu.VMEM)
SMEM = pl.BlockSpec(memory_space=pltpu.SMEM)


def shape(*dims):
    return jax.ShapeDtypeStruct(dims, F32)


def call(kernel, outs, smem_count, args, scratch=(), flops=10**7):
    nbytes = 4 * sum(a.size for a in args) + 4 * sum(o.size for o in outs)
    return pl.pallas_call(
        kernel,
        out_shape=tuple(outs),
        in_specs=[SMEM] * smem_count + [VMEM] * (len(args) - smem_count),
        out_specs=tuple(VMEM for _ in outs),
        scratch_shapes=list(scratch),
        compiler_params=pltpu.CompilerParams(vmem_limit_bytes=24 * 1024 * 1024),
        cost_estimate=pl.CostEstimate(flops=flops, bytes_accessed=nbytes, transcendentals=0),
    )(*args)


def ring(value, axis, shift):
    count = lax.axis_size(axis)
    return lax.ppermute(value, axis, [(i, (i + shift) % count) for i in range(count)])


def up_depth(value, shift, lane):
    if shift == 0:
        return value
    rolled = pltpu.roll(value, (-shift) % NZ, 1)
    keep = lane < NZ - shift if shift > 0 else lane >= -shift
    return jnp.where(keep, rolled, 0.0)


def plus(take):
    summed = coeffs[0] * (take(1) - take(0))
    for r in (2, 3, 4):
        summed = summed + coeffs[r - 1] * (take(r) - take(1 - r))
    return summed


def minus(take):
    summed = coeffs[0] * (take(0) - take(-1))
    for r in (2, 3, 4):
        summed = summed + coeffs[r - 1] * (take(r - 1) - take(-r))
    return summed


def step_kernel(moment, forward, last, off_p, off_v, row_p, row_v, *refs):
    refs = list(refs)
    take = refs.pop
    ints = take(0)
    amps = take(0) if forward else None
    press, pxl, pxh, pyl, pyh = [take(0) for _ in range(5)]
    vel, vxl, vxh, vyl, vyh = [take(0) for _ in range(5)]
    buoy, bxl, bxh, byl, byh, modu = [take(0) for _ in range(6)]
    if forward:
        count, obs = take(0), take(0)
        back = take(0) if last else None
    else:
        div_in, slope_in = take(0), take(0)
        gm_in, gb_in = (None, None) if moment == STEPS - 1 else (take(0), take(0))
        inject = None if last else take(0)
    if forward:
        div_out, slope_out = take(0), take(0)
        inject_out = None if last else take(0)
    else:
        gm_out, gb_out = take(0), take(0)
    ends = forward or not last
    if ends:
        p_out, sxl, sxh, syl, syh = [take(0) for _ in range(5)]
    if not last:
        vel_out, vxl_out, vxh_out, vyl_out, vyh_out = [take(0) for _ in range(5)]
    wide, vx, tall, vy_tall, vz_all = [take(0) for _ in range(5)]

    low_x = ints[0].astype(F32)
    high_x = ints[1].astype(F32)
    low_y = ints[2].astype(F32)
    high_y = ints[3].astype(F32)
    for i in range(HP):
        wide[i] = pxl[off_p + i] * low_x
        wide[HP + NXT + i] = pxh[off_p + i] * high_x

    nothing = jnp.zeros((8, NZ), F32)

    def copy(x, carry):
        here = press[x]
        wide[x + HP] = here
        tall[x, 0:8] = nothing
        tall[x, 8:16] = pyl[x, row_p : row_p + 8] * low_y
        tall[x, 16:48] = here
        tall[x, 48:56] = pyh[x, row_p : row_p + 8] * high_y
        tall[x, 56:64] = nothing
        vy_tall[x, 0:8] = nothing
        vy_tall[x, 56:64] = nothing
        return carry

    lax.fori_loop(0, NXT, copy, 0, unroll=UNROLL[0])

    def slope_x(i):
        return plus(lambda s: wide[i + 3 + s])

    for i in range(HV):
        vx[i] = low_x * (vxl[off_v + i] - bxl[i] * slope_x(i))
        if not last:
            vxl_out[i] = vx[i]
    for i in range(HV - 1):
        at = HV + NXT + i
        vx[at] = high_x * (vxh[off_v + i] - bxh[i] * slope_x(at))
        if not last:
            vxh_out[i] = vx[at]
    if not last:
        vxh_out[HV - 1] = jnp.zeros((NYT, NZ), F32)

    lane = lax.broadcasted_iota(jnp.int32, (NYT, NZ), 1)

    def first(x, carry):
        b_here = buoy[x]
        slope = slope_x(x + HV)
        new = vel[0, x] - b_here * slope
        vx[x + HV] = new
        slope_y = plus(lambda s: tall[x, 8 + s : 56 + s])
        vy_low = low_y * (vyl[x, row_v : row_v + 8] - byl[x] * slope_y[0:8])
        vy = vel[1, x] - b_here * slope_y[8:40]
        vy_high = high_y * (vyh[x, row_v : row_v + 8] - byh[x] * slope_y[40:48])
        vy_tall[x, 8:16] = vy_low
        vy_tall[x, 16:48] = vy
        vy_tall[x, 48:56] = vy_high
        slope_z = plus(lambda s: up_depth(press[x], s, lane))
        vz = vel[2, x] - b_here * slope_z
        vz_all[x] = vz
        if not last:
            vel_out[0, x] = new
            vel_out[1, x] = vy
            vel_out[2, x] = vz
            vyl_out[x] = vy_low
            vyh_out[x] = vy_high
        if forward:
            slope_out[0, x] = slope
            slope_out[1, x] = slope_y[8:40]
            slope_out[2, x] = slope_z
        return carry

    lax.fori_loop(0, NXT, first, 0, unroll=UNROLL[1])

    if forward:
        cell = lax.broadcasted_iota(jnp.int32, (NYT, NZ), 0) * NZ + lane
        source_x = ints[4]
        source_at = ints[5] * NZ + ints[6]
        amplitude = amps[moment, 0]

    def second(x, carry):
        here = press[x]
        vz = vz_all[x]
        diverge = minus(lambda s: vx[x + HV + s])
        diverge = diverge + minus(lambda s: vy_tall[x, 16 + s : 48 + s])
        diverge = diverge + minus(lambda s: up_depth(vz, s, lane))
        new = here - modu[x] * diverge
        if forward:
            div_out[x] = diverge
            at = jnp.where(x == source_x, source_at, -1)
            new = new + jnp.where(cell == at, amplitude, 0.0)
            misfit = count[x] * new - obs[moment, x]
            if last:
                new = back[x] + misfit
            else:
                inject_out[x] = misfit
        else:
            part_m = new * div_in[x]
            part_b = vx[x + HV] * slope_in[0, x] + vy_tall[x, 16:48] * slope_in[1, x] + vz * slope_in[2, x]
            if gm_in is None:
                gm_out[x] = -part_m
                gb_out[x] = -part_b
            else:
                gm_out[x] = gm_in[x] - part_m
                gb_out[x] = gb_in[x] - part_b
            if not last:
                new = new + inject[x]
        if ends:
            p_out[x] = new
            syl[x] = new[0:8]
            syh[x] = new[24:32]
        return carry

    lax.fori_loop(0, NXT, second, 0, unroll=UNROLL[2])
    if ends:
        for i in range(HP):
            sxl[i] = p_out[i]
            sxh[i] = p_out[NXT - HP + i]


def step(moment, forward, last, offsets, ints, amps, press, vel, material, extra):
    tile = shape(NXT, NYT, NZ)
    three = shape(3, NXT, NYT, NZ)
    beside_y = shape(NXT, 8, NZ)
    outs = [tile, three if forward else tile]
    if forward and not last:
        outs.append(tile)
    if forward or not last:
        outs += [tile, shape(HP, NYT, NZ), shape(HP, NYT, NZ), beside_y, beside_y]
    if not last:
        outs += [three, shape(HV, NYT, NZ), shape(HV, NYT, NZ), beside_y, beside_y]
    scalars = [ints, amps] if forward else [ints]
    args = scalars + list(press) + list(vel) + list(material) + list(extra)
    scratch = [
        pltpu.VMEM(dims, F32)
        for dims in (
            (NXT + 2 * HP, NYT, NZ),
            (NXT + 2 * HV, NYT, NZ),
            (NXT, NYT + 32, NZ),
            (NXT, NYT + 32, NZ),
            (NXT, NYT, NZ),
        )
    ]
    kernel = functools.partial(step_kernel, moment, forward, last, *offsets)
    return call(kernel, outs, len(scalars), args, scratch)


def exchange(low_x, high_x, low_y, high_y):
    return (
        ring(high_x, "gx", 1),
        ring(low_x, "gx", -1),
        ring(high_y, "gy", 1),
        ring(low_y, "gy", -1),
    )


def spread_rows():
    row = lax.broadcasted_iota(jnp.int32, (64, 2 * NZ), 0)
    lane = lax.broadcasted_iota(jnp.int32, (64, 2 * NZ), 1)
    same = ((row >> 2) & 1) == (lane >> 7)
    depth = (row >> 3) * 4 + (row & 3)
    return jnp.where(same & (((lane & 127) >> 2) == depth), 1.0, 0.0).astype(BF16)


def split(value):
    high = value.astype(BF16)
    return high, (value - high.astype(F32)).astype(BF16)


def dot(a, b, dims=((1,), (0,))):
    return lax.dot_general(a, b, (dims, ((), ())), preferred_element_type=F32)


def stack_right(value):
    high, low = split(value)
    return jnp.concatenate([high, high, low], axis=0)


def dot_rows(a, b):
    dims = ((1,), (1,))
    return dot(a[0], b[0], dims) + (dot(a[0], b[1], dims) + dot(a[1], b[0], dims))


def phases(dtype):
    lane = lax.broadcasted_iota(jnp.int32, (64, 2 * NZ), 1) & 3
    return [jnp.where(lane == k, 1.0, 0.0).astype(dtype) for k in range(4)]


def decode_kernel(mix_first, mix_second, blocks, *refs):
    modu, buoy, bxl, bxh, byl, byh, sig_speed, sig_dens, latent_out, hidden_out = refs
    spread = spread_rows()
    spread = jnp.concatenate([spread, spread, spread], axis=0)
    phase = lax.broadcasted_iota(jnp.int32, (64, 2 * NZ), 1) & 3
    for g in range(GROUPS):
        a, half = divmod(g, 2)
        rows = blocks[:, 8 * g : 8 * g + 8, :].reshape(64, 128)
        high, rest = rows.astype(BF16), None
        rest = rows - high.astype(F32)
        middle, low = split(rest)
        pieces = jnp.concatenate([high, middle, low], axis=0)
        latent = dot(pieces, spread, ((0,), (0,)))
        hidden = jnp.tanh(dot(mix_first[...], stack_right(latent)))
        latent_out[g] = latent
        hidden_out[g] = hidden
        out = dot(mix_second[...], stack_right(hidden))
        fine = out[0:64]
        for k in (1, 2, 3):
            fine = jnp.where(phase == k, out[64 * k : 64 * k + 64], fine)
        sig = jax.nn.sigmoid(fine)
        s1, s2 = sig[0:32], sig[32:64]
        speed = 0.15 + 0.25 * s1
        dens = 1.0 + 1.5 * s2
        mod = dens * speed * speed
        inv = 1.0 / dens
        for i in range(4):
            for q in range(2):
                x = 4 * a + i
                ys = slice(16 * half + 8 * q, 16 * half + 8 * q + 8)
                part = (slice(8 * i, 8 * i + 8), slice(NZ * q, NZ * q + NZ))
                sig_speed[x, ys] = s1[part]
                sig_dens[x, ys] = s2[part]
                modu[x, ys] = mod[part]
                buoy[x, ys] = inv[part]
    for i in range(HV):
        bxl[i] = buoy[i]
        bxh[i] = buoy[NXT - HV + i]
    byl[...] = buoy[:, 0:8, :]
    byh[...] = buoy[:, 24:32, :]


def grads_kernel(
    back_first, back_second, order, gm, gb, sig_speed, sig_dens, latent_in, hidden_in, *refs
):
    send, second_sum, first_sum = refs
    spread = spread_rows()
    spread = jnp.concatenate([spread, spread], axis=1)
    masks = phases(BF16)

    def square(field, a, half):
        return jnp.concatenate(
            [
                jnp.concatenate(
                    [field[4 * a + i, 16 * half + 8 * q : 16 * half + 8 * q + 8] for i in range(4)],
                    axis=0,
                )
                for q in range(2)
            ],
            axis=1,
        )

    for g in range(GROUPS):
        a, half = divmod(g, 2)
        s1, s2 = square(sig_speed, a, half), square(sig_dens, a, half)
        g_mod, g_buoy = square(gm, a, half), square(gb, a, half)
        speed = 0.15 + 0.25 * s1
        dens = 1.0 + 1.5 * s2
        grad_speed = g_mod * 2.0 * dens * speed
        grad_dens = g_mod * speed * speed - g_buoy / (dens * dens)
        fine = jnp.concatenate(
            [grad_speed * 0.25 * s1 * (1.0 - s1), grad_dens * 1.5 * s2 * (1.0 - s2)], axis=0
        )
        high, low = split(fine)
        high = jnp.concatenate([high * mask for mask in masks], axis=0)
        low = jnp.concatenate([low * mask for mask in masks], axis=0)
        latent, hidden = latent_in[g], hidden_in[g]
        grad_hidden = dot(back_second[...], jnp.concatenate([high, high, low], axis=0))
        grad_pre = grad_hidden * (1.0 - hidden * hidden)
        pre = split(grad_pre)
        grad_latent = dot(back_first[...], jnp.concatenate([pre[0], pre[0], pre[1]], axis=0))
        gathered = dot(
            spread, jnp.concatenate(split(grad_latent), axis=1), ((1,), (1,))
        )
        for j in range(8):
            send[j, 8 * g : 8 * g + 8, :] = gathered[8 * j : 8 * j + 8]
        second = dot_rows(split(hidden), (high, low))
        first = dot_rows(split(latent), pre)
        if g == 0:
            second_sum[...] = second
            first_sum[...] = first
        else:
            second_sum[...] += second
            first_sum[...] += first
    column = lax.broadcasted_iota(jnp.int32, (CH, 256), 1)
    total = jnp.where(((column >> 2) & 1) == 0, second_sum[0:64], second_sum[64:128])
    total = lax.dot_general(
        total, order[...], (((1,), (0,)), ((), ())), precision=HI, preferred_element_type=F32
    )
    corner = first_sum[0:64, 0:64] + first_sum[64:128, 64:128]
    packed = jnp.concatenate(
        [total, jnp.concatenate([corner[0:32], corner[32:64]], axis=1)], axis=0
    )
    for j in range(8):
        send[j, 96:108, :] = packed[12 * j : 12 * j + 12]


def sum_kernel(*refs):
    parts, latent_out, weights_out = refs
    total = parts[0]
    for j in range(1, 8):
        total = total + parts[j]
    for q in range(24):
        a, t = divmod(q, 4)
        for c in range(4):
            latent_out[c, a : a + 1, 128 * t : 128 * t + 128] = total[4 * q + c : 4 * q + c + 1]
    weights_out[...] = total[96:108]


def receiver_fields(rec_pos, observed, anchor_x, anchor_y):
    local_x = rec_pos[0] - anchor_x
    local_y = rec_pos[1] - anchor_y
    inside = (local_x >= 0) & (local_x < NXT) & (local_y >= 0) & (local_y < NYT)
    row = jnp.where(inside, local_x * NYT + local_y, -1)
    rows = (lax.broadcasted_iota(jnp.int32, (NXT * NYT, row.shape[0]), 0) == row).astype(
        jnp.bfloat16
    )
    coarse = lax.reduce_precision(observed, 8, 7)
    rest = observed - coarse
    values = jnp.concatenate([jnp.ones((1, row.shape[0]), F32), coarse, rest], axis=0)
    hit = lax.broadcasted_iota(jnp.int32, (row.shape[0], NZ), 1) == rec_pos[2][:, None]
    spread = jnp.where(hit[:, None, :], values.T[:, :, None], 0.0).astype(jnp.bfloat16)
    fields = jnp.dot(
        rows, spread.reshape(row.shape[0], 7 * NZ), preferred_element_type=F32
    ).reshape(NXT, NYT, 7, NZ)
    fields = fields.transpose(2, 0, 1, 3)
    return fields[0], fields[1:4] + fields[4:7]


def body(
    latent,
    w_first,
    w_second,
    fwd_press,
    fwd_vel,
    adj_press,
    adj_vel,
    src_pos,
    src_amp,
    rec_pos,
    observed,
):
    at_x, at_y = lax.axis_index("gx"), lax.axis_index("gy")
    anchor_x, anchor_y = at_x * NXT, at_y * NYT
    source_x, source_y = src_pos[0, 0] - anchor_x, src_pos[1, 0] - anchor_y
    inside = (source_x >= 0) & (source_x < NXT) & (source_y >= 0) & (source_y < NYT)
    ints = jnp.stack(
        [
            at_x > 0,
            at_x < lax.axis_size("gx") - 1,
            at_y > 0,
            at_y < lax.axis_size("gy") - 1,
            jnp.where(inside, source_x, -1),
            source_y,
            src_pos[2, 0],
            inside,
        ]
    ).astype(jnp.int32)

    flat = latent.reshape(4, 24, 128).transpose(1, 0, 2).reshape(96, 128)
    blocks = lax.all_to_all(jnp.broadcast_to(flat, (8, 96, 128)), "shot", 0, 0, tiled=True)

    press, back_press = fwd_press[0], adj_press[0]
    vel, back_vel = fwd_vel[0], adj_vel[0]
    beside = exchange(
        jnp.concatenate([press[:HP], vel[0, :HV], back_vel[0, :HV]], axis=0),
        jnp.concatenate([press[-HP:], vel[0, -HV:], back_vel[0, -HV:]], axis=0),
        jnp.concatenate([press[:, :8], vel[1, :, :8], back_vel[1, :, :8]], axis=1),
        jnp.concatenate([press[:, -8:], vel[1, :, -8:], back_vel[1, :, -8:]], axis=1),
    )
    count, obs = receiver_fields(rec_pos[0], observed[0], anchor_x, anchor_y)

    same = jnp.eye(2, dtype=F32)
    mix_first = (same[:, None, :, None] * w_first.T[None, :, None, :]).reshape(128, 128)
    by_phase = w_second.reshape(CH, 2, 4, 4, 4).transpose(4, 1, 2, 3, 0)
    mix_second = (
        by_phase[:, :, :, None, :, None, :] * same[None, None, None, :, None, :, None]
    ).reshape(256, 128)
    column = lax.broadcasted_iota(jnp.int32, (256, 128), 0)
    natural = (((column >> 3) & 7) << 4) + ((column & 3) << 2) + (column >> 6)
    order = (natural == lax.broadcasted_iota(jnp.int32, (256, 128), 1)).astype(F32)

    def stack_left(matrix):
        high = lax.reduce_precision(matrix, 8, 7)
        return jnp.concatenate([high, matrix - high, high], axis=1).astype(BF16)

    tile = shape(NXT, NYT, NZ)
    beside_x, beside_y = shape(HV, NYT, NZ), shape(NXT, 8, NZ)
    decoded = call(
        decode_kernel,
        [tile, tile, beside_x, beside_x, beside_y, beside_y, tile, tile]
        + [shape(GROUPS, 128, 2 * NZ)] * 2,
        0,
        [stack_left(mix_first), stack_left(mix_second), blocks],
    )
    modulus, buoyancy = decoded[:2]
    material = (buoyancy,) + exchange(*decoded[2:6]) + (modulus,)
    sig_speed, sig_dens, latent_wide, hidden_wide = decoded[6:]

    stored, injects = [], []
    state_p = (press,) + beside
    state_v = (vel,) + beside
    offsets = (0, HP, 0, 8)
    for moment in range(STEPS):
        last = moment == STEPS - 1
        extra = [count, obs] + ([back_press] if last else [])
        outs = step(
            moment, True, last, offsets, ints, src_amp, state_p, state_v, material, extra
        )
        stored.append(outs[:2])
        outs = outs[2:]
        if not last:
            injects.append(outs[0])
            outs = outs[1:]
            state_v = outs[5:]
        state_p = (outs[0],) + exchange(*outs[1:5])
        offsets = (0, 0, 0, 0)
    state_v = (back_vel,) + beside
    offsets = (0, HP + HV, 0, 16)
    sums = []
    for moment in reversed(range(STEPS)):
        last = moment == 0
        extra = list(stored[moment]) + sums + ([] if last else [injects[moment - 1]])
        outs = step(moment, False, last, offsets, ints, None, state_p, state_v, material, extra)
        sums = list(outs[:2])
        if not last:
            state_p = (outs[2],) + exchange(*outs[3:7])
            state_v = outs[7:]
        offsets = (0, 0, 0, 0)

    (send,) = call(
        grads_kernel,
        [shape(8, 108, 128)],
        0,
        [stack_left(mix_first.T), stack_left(mix_second.T), order] + sums
        + [sig_speed, sig_dens, latent_wide, hidden_wide],
        [pltpu.VMEM((128, 256), F32), pltpu.VMEM((128, 128), F32)],
    )
    parts = lax.all_to_all(send, "shot", 0, 0, tiled=True)
    grad_latent, weights = call(sum_kernel, [shape(4, 6, 512), shape(12, 128)], 0, [parts])
    group = lax.axis_size("gx") * lax.axis_size("gy")
    weights = lax.all_to_all(
        jnp.broadcast_to(weights, (group, 12, 128)), ("gx", "gy"), 0, 0, tiled=True
    )
    weights = jnp.sum(weights, axis=0)
    weights = lax.all_to_all(jnp.broadcast_to(weights, (8, 12, 128)), "shot", 0, 0, tiled=True)
    weights = weights.reshape(96, 128)
    grad_second = weights[:64]
    grad_first = jnp.concatenate([weights[64:, :64], weights[64:, 64:]], axis=0)
    return (grad_latent, grad_first, grad_second)


def solution(mesh):
    in_specs = (
        P("shot", "gx", "gy"),
        P(),
        P(),
        P("shot", "gx", "gy", None),
        P("shot", None, "gx", "gy", None),
        P("shot", "gx", "gy", None),
        P("shot", None, "gx", "gy", None),
        P(None, "shot"),
        P(None, "shot"),
        P("shot", None, None),
        P("shot", None, None),
    )
    out_specs = (P("shot", "gx", "gy"), P(), P())
    return jax.shard_map(body, mesh=mesh, in_specs=in_specs, out_specs=out_specs, check_vma=False)
```

```python
import functools

import jax
import jax.numpy as jnp
from jax import lax
from jax.experimental import pallas as pl
from jax.experimental.pallas import tpu as pltpu
from jax.sharding import PartitionSpec as P

CH = 64
STEPS = 3
coeffs = (1225.0 / 1024.0, -245.0 / 3072.0, 49.0 / 5120.0, -5.0 / 7168.0)

NXT, NYT, NZ = 24, 32, 128
GROUPS = 12
HP = 7
HV = 4
HI = lax.Precision.HIGHEST
F32 = jnp.float32
BF16 = jnp.bfloat16
UNROLL = (8, 8, 8)
VMEM = pl.BlockSpec(memory_space=pltpu.VMEM)
SMEM = pl.BlockSpec(memory_space=pltpu.SMEM)


def shape(*dims):
    return jax.ShapeDtypeStruct(dims, F32)


def call(kernel, outs, smem_count, args, scratch=(), flops=10**7):
    nbytes = 4 * sum(a.size for a in args) + 4 * sum(o.size for o in outs)
    return pl.pallas_call(
        kernel,
        out_shape=tuple(outs),
        in_specs=[SMEM] * smem_count + [VMEM] * (len(args) - smem_count),
        out_specs=tuple(VMEM for _ in outs),
        scratch_shapes=list(scratch),
        compiler_params=pltpu.CompilerParams(vmem_limit_bytes=16 * 1024 * 1024),
        cost_estimate=pl.CostEstimate(flops=flops, bytes_accessed=nbytes, transcendentals=0),
    )(*args)


def ring(value, axis, shift):
    count = lax.axis_size(axis)
    return lax.ppermute(value, axis, [(i, (i + shift) % count) for i in range(count)])


def up_depth(value, shift, lane):
    if shift == 0:
        return value
    rolled = pltpu.roll(value, (-shift) % NZ, 1)
    keep = lane < NZ - shift if shift > 0 else lane >= -shift
    return jnp.where(keep, rolled, 0.0)


def plus(take):
    summed = coeffs[0] * (take(1) - take(0))
    for r in (2, 3, 4):
        summed = summed + coeffs[r - 1] * (take(r) - take(1 - r))
    return summed


def minus(take):
    summed = coeffs[0] * (take(0) - take(-1))
    for r in (2, 3, 4):
        summed = summed + coeffs[r - 1] * (take(r - 1) - take(-r))
    return summed


def step_kernel(moment, forward, last, off_p, off_v, row_p, row_v, *refs):
    refs = list(refs)
    take = refs.pop
    source, amps = (take(0), take(0)) if forward else (None, None)
    press, pxl, pxh, pyl, pyh = [take(0) for _ in range(5)]
    vel, vxl, vxh, vyl, vyh = [take(0) for _ in range(5)]
    buoy, bxl, bxh, byl, byh, modu = [take(0) for _ in range(6)]
    if forward:
        count, obs, back = (take(0), take(0), take(0)) if last else (None, None, None)
    else:
        div_in, slope_in = take(0), take(0)
        gm_in, gb_in = (None, None) if moment == STEPS - 1 else (take(0), take(0))
        count, obs, earlier = (None, None, None) if last else (take(0), take(0), take(0))
    if forward:
        div_out, slope_out = take(0), take(0)
    else:
        gm_out, gb_out = take(0), take(0)
    ends = forward or not last
    if ends:
        p_out, sxl, sxh, syl, syh = [take(0) for _ in range(5)]
    if not last:
        vel_out, vxl_out, vxh_out, vyl_out, vyh_out = [take(0) for _ in range(5)]
    wide, vx, tall, vy_tall, vz_all = [take(0) for _ in range(5)]

    at_x, at_y = lax.axis_index("gx"), lax.axis_index("gy")
    low_x = jnp.where(at_x > 0, 1.0, 0.0)
    high_x = jnp.where(at_x < lax.axis_size("gx") - 1, 1.0, 0.0)
    low_y = jnp.where(at_y > 0, 1.0, 0.0)
    high_y = jnp.where(at_y < lax.axis_size("gy") - 1, 1.0, 0.0)
    for i in range(HP):
        wide[i] = pxl[off_p + i] * low_x
        wide[HP + NXT + i] = pxh[off_p + i] * high_x

    nothing = jnp.zeros((8, NZ), F32)

    def copy(x, carry):
        here = press[x]
        wide[x + HP] = here
        tall[x, 0:8] = nothing
        tall[x, 8:16] = pyl[x, row_p : row_p + 8] * low_y
        tall[x, 16:48] = here
        tall[x, 48:56] = pyh[x, row_p : row_p + 8] * high_y
        tall[x, 56:64] = nothing
        vy_tall[x, 0:8] = nothing
        vy_tall[x, 56:64] = nothing
        return carry

    lax.fori_loop(0, NXT, copy, 0, unroll=UNROLL[0])

    def slope_x(i):
        return plus(lambda s: wide[i + 3 + s])

    for i in range(HV):
        vx[i] = low_x * (vxl[off_v + i] - bxl[i] * slope_x(i))
        if not last:
            vxl_out[i] = vx[i]
    for i in range(HV - 1):
        at = HV + NXT + i
        vx[at] = high_x * (vxh[off_v + i] - bxh[i] * slope_x(at))
        if not last:
            vxh_out[i] = vx[at]
    if not last:
        vxh_out[HV - 1] = jnp.zeros((NYT, NZ), F32)

    lane = lax.broadcasted_iota(jnp.int32, (NYT, NZ), 1)

    def first(x, carry):
        b_here = buoy[x]
        slope = slope_x(x + HV)
        new = vel[0, x] - b_here * slope
        vx[x + HV] = new
        slope_y = plus(lambda s: tall[x, 8 + s : 56 + s])
        vy_low = low_y * (vyl[x, row_v : row_v + 8] - byl[x] * slope_y[0:8])
        vy = vel[1, x] - b_here * slope_y[8:40]
        vy_high = high_y * (vyh[x, row_v : row_v + 8] - byh[x] * slope_y[40:48])
        vy_tall[x, 8:16] = vy_low
        vy_tall[x, 16:48] = vy
        vy_tall[x, 48:56] = vy_high
        slope_z = plus(lambda s: up_depth(press[x], s, lane))
        vz = vel[2, x] - b_here * slope_z
        vz_all[x] = vz
        if not last:
            vel_out[0, x] = new
            vel_out[1, x] = vy
            vel_out[2, x] = vz
            vyl_out[x] = vy_low
            vyh_out[x] = vy_high
        if forward:
            slope_out[0, x] = slope
            slope_out[1, x] = slope_y[8:40]
            slope_out[2, x] = slope_z
        return carry

    lax.fori_loop(0, NXT, first, 0, unroll=UNROLL[1])

    if forward:
        cell = lax.broadcasted_iota(jnp.int32, (NYT, NZ), 0) * NZ + lane
        source_x = source[0] - at_x * NXT
        source_y = source[1] - at_y * NYT
        source_at = jnp.where((source_y >= 0) & (source_y < NYT), source_y * NZ + source[2], -1)
        amplitude = amps[moment]

    def second(x, carry):
        here = press[x]
        vz = vz_all[x]
        diverge = minus(lambda s: vx[x + HV + s])
        diverge = diverge + minus(lambda s: vy_tall[x, 16 + s : 48 + s])
        diverge = diverge + minus(lambda s: up_depth(vz, s, lane))
        new = here - modu[x] * diverge
        if forward:
            div_out[x] = diverge
            at = jnp.where(x == source_x, source_at, -1)
            new = new + jnp.where(cell == at, amplitude, 0.0)
            if last:
                new = back[x] + (count[x] * new - obs[moment, x])
        else:
            part_m = new * div_in[x]
            part_b = vx[x + HV] * slope_in[0, x] + vy_tall[x, 16:48] * slope_in[1, x] + vz * slope_in[2, x]
            if gm_in is None:
                gm_out[x] = -part_m
                gb_out[x] = -part_b
            else:
                gm_out[x] = gm_in[x] - part_m
                gb_out[x] = gb_in[x] - part_b
            if not last:
                new = new + (count[x] * earlier[x] - obs[moment - 1, x])
        if ends:
            p_out[x] = new
            syl[x] = new[0:8]
            syh[x] = new[24:32]
        return carry

    lax.fori_loop(0, NXT, second, 0, unroll=UNROLL[2])
    if ends:
        for i in range(HP):
            sxl[i] = p_out[i]
            sxh[i] = p_out[NXT - HP + i]


def step(moment, forward, last, offsets, scalars, press, vel, material, extra):
    tile = shape(NXT, NYT, NZ)
    three = shape(3, NXT, NYT, NZ)
    beside_y = shape(NXT, 8, NZ)
    outs = [tile, three if forward else tile]
    if forward or not last:
        outs += [tile, shape(HP, NYT, NZ), shape(HP, NYT, NZ), beside_y, beside_y]
    if not last:
        outs += [three, shape(HV, NYT, NZ), shape(HV, NYT, NZ), beside_y, beside_y]
    args = list(scalars) + list(press) + list(vel) + list(material) + list(extra)
    scratch = [
        pltpu.VMEM(dims, F32)
        for dims in (
            (NXT + 2 * HP, NYT, NZ),
            (NXT + 2 * HV, NYT, NZ),
            (NXT, NYT + 32, NZ),
            (NXT, NYT + 32, NZ),
            (NXT, NYT, NZ),
        )
    ]
    kernel = functools.partial(step_kernel, moment, forward, last, *offsets)
    return call(kernel, outs, len(scalars), args, scratch)


def exchange(low_x, high_x, low_y, high_y):
    return (
        ring(high_x, "gx", 1),
        ring(low_x, "gx", -1),
        ring(high_y, "gy", 1),
        ring(low_y, "gy", -1),
    )


def spread_rows():
    row = lax.broadcasted_iota(jnp.int32, (64, 2 * NZ), 0)
    lane = lax.broadcasted_iota(jnp.int32, (64, 2 * NZ), 1)
    same = ((row >> 2) & 1) == (lane >> 7)
    depth = (row >> 3) * 4 + (row & 3)
    return jnp.where(same & (((lane & 127) >> 2) == depth), 1.0, 0.0).astype(BF16)


def split(value):
    high = value.astype(BF16)
    return high, (value - high.astype(F32)).astype(BF16)


def dot(a, b, dims=((1,), (0,))):
    return lax.dot_general(a, b, (dims, ((), ())), preferred_element_type=F32)


def stack_right(value):
    high, low = split(value)
    return jnp.concatenate([high, high, low], axis=0)


def dot_rows(a, b):
    dims = ((1,), (1,))
    return dot(a[0], b[0], dims) + (dot(a[0], b[1], dims) + dot(a[1], b[0], dims))


def reorder():
    row = lax.broadcasted_iota(jnp.int32, (256, 128), 0)
    natural = (((row >> 3) & 7) << 4) + ((row & 3) << 2) + (row >> 6)
    picked = natural == lax.broadcasted_iota(jnp.int32, (256, 128), 1)
    return jnp.where(picked, 1.0, 0.0)


def two_blocks(matrix):
    empty = jnp.zeros((CH, CH), F32)
    return jnp.concatenate(
        [jnp.concatenate([matrix, empty], axis=1), jnp.concatenate([empty, matrix], axis=1)],
        axis=0,
    )


def stack_left(matrix):
    high, low = split(matrix)
    return jnp.concatenate([high, low, high], axis=1)


def phases(dtype):
    lane = lax.broadcasted_iota(jnp.int32, (64, 2 * NZ), 1) & 3
    return [jnp.where(lane == k, 1.0, 0.0).astype(dtype) for k in range(4)]


def decode_kernel(w_first, w_second, blocks, *refs):
    modu, buoy, bxl, bxh, byl, byh, sig_speed, sig_dens, latent_out, hidden_out = refs
    spread = spread_rows()
    spread = jnp.concatenate([spread, spread, spread], axis=0)
    phase = lax.broadcasted_iota(jnp.int32, (64, 2 * NZ), 1) & 3
    mix_first = stack_left(two_blocks(w_first[...]).T)
    chosen = reorder().astype(BF16)
    cell = (lax.broadcasted_iota(jnp.int32, (256, CH), 0) >> 2) & 1
    pieces = []
    for piece in split(w_second[...]):
        rows = dot(chosen, piece, ((1,), (1,)))
        pieces.append(
            jnp.concatenate([jnp.where(cell == b, rows, 0.0) for b in range(2)], axis=1)
        )
    pieces = [piece.astype(BF16) for piece in pieces]
    mix_second = jnp.concatenate([pieces[0], pieces[1], pieces[0]], axis=1)
    for g in range(GROUPS):
        a, half = divmod(g, 2)
        rows = blocks[:, 8 * g : 8 * g + 8, :].reshape(64, 128)
        high, rest = rows.astype(BF16), None
        rest = rows - high.astype(F32)
        middle, low = split(rest)
        pieces = jnp.concatenate([high, middle, low], axis=0)
        latent = dot(pieces, spread, ((0,), (0,)))
        hidden = jnp.tanh(dot(mix_first, stack_right(latent)))
        latent_out[g] = latent
        hidden_out[g] = hidden
        out = dot(mix_second, stack_right(hidden))
        fine = out[0:64]
        for k in (1, 2, 3):
            fine = jnp.where(phase == k, out[64 * k : 64 * k + 64], fine)
        sig = jax.nn.sigmoid(fine)
        s1, s2 = sig[0:32], sig[32:64]
        speed = 0.15 + 0.25 * s1
        dens = 1.0 + 1.5 * s2
        mod = dens * speed * speed
        inv = 1.0 / dens
        for i in range(4):
            for q in range(2):
                x = 4 * a + i
                ys = slice(16 * half + 8 * q, 16 * half + 8 * q + 8)
                part = (slice(8 * i, 8 * i + 8), slice(NZ * q, NZ * q + NZ))
                sig_speed[x, ys] = s1[part]
                sig_dens[x, ys] = s2[part]
                modu[x, ys] = mod[part]
                buoy[x, ys] = inv[part]
    for i in range(HV):
        bxl[i] = buoy[i]
        bxh[i] = buoy[NXT - HV + i]
    byl[...] = buoy[:, 0:8, :]
    byh[...] = buoy[:, 24:32, :]


def grads_kernel(
    w_first, w_second, gm, gb, sig_speed, sig_dens, latent_in, hidden_in, *refs
):
    send, second_sum, first_sum = refs
    spread = spread_rows()
    spread = jnp.concatenate([spread, spread], axis=1)
    masks = phases(BF16)
    back_first = stack_left(two_blocks(w_first[...]))
    order = reorder()
    chosen = order.astype(BF16)
    cell = (lax.broadcasted_iota(jnp.int32, (CH, 256), 1) >> 2) & 1
    pieces = []
    for piece in split(w_second[...]):
        columns = dot(piece, chosen, ((1,), (1,)))
        pieces.append(
            jnp.concatenate([jnp.where(cell == b, columns, 0.0) for b in range(2)], axis=0)
        )
    pieces = [piece.astype(BF16) for piece in pieces]
    back_second = jnp.concatenate([pieces[0], pieces[1], pieces[0]], axis=1)

    def square(field, a, half):
        return jnp.concatenate(
            [
                jnp.concatenate(
                    [field[4 * a + i, 16 * half + 8 * q : 16 * half + 8 * q + 8] for i in range(4)],
                    axis=0,
                )
                for q in range(2)
            ],
            axis=1,
        )

    for g in range(GROUPS):
        a, half = divmod(g, 2)
        s1, s2 = square(sig_speed, a, half), square(sig_dens, a, half)
        g_mod, g_buoy = square(gm, a, half), square(gb, a, half)
        speed = 0.15 + 0.25 * s1
        dens = 1.0 + 1.5 * s2
        grad_speed = g_mod * 2.0 * dens * speed
        grad_dens = g_mod * speed * speed - g_buoy / (dens * dens)
        fine = jnp.concatenate(
            [grad_speed * 0.25 * s1 * (1.0 - s1), grad_dens * 1.5 * s2 * (1.0 - s2)], axis=0
        )
        high, low = split(fine)
        high = jnp.concatenate([high * mask for mask in masks], axis=0)
        low = jnp.concatenate([low * mask for mask in masks], axis=0)
        latent, hidden = latent_in[g], hidden_in[g]
        grad_hidden = dot(back_second, jnp.concatenate([high, high, low], axis=0))
        grad_pre = grad_hidden * (1.0 - hidden * hidden)
        pre = split(grad_pre)
        grad_latent = dot(back_first, jnp.concatenate([pre[0], pre[0], pre[1]], axis=0))
        gathered = dot(
            spread, jnp.concatenate(split(grad_latent), axis=1), ((1,), (1,))
        )
        for j in range(8):
            send[j, 8 * g : 8 * g + 8, :] = gathered[8 * j : 8 * j + 8]
        second = dot_rows(split(hidden), (high, low))
        first = dot_rows(split(latent), pre)
        if g == 0:
            second_sum[...] = second
            first_sum[...] = first
        else:
            second_sum[...] += second
            first_sum[...] += first
    column = lax.broadcasted_iota(jnp.int32, (CH, 256), 1)
    total = jnp.where(((column >> 2) & 1) == 0, second_sum[0:64], second_sum[64:128])
    total = lax.dot_general(
        total, order, (((1,), (0,)), ((), ())), precision=HI, preferred_element_type=F32
    )
    corner = first_sum[0:64, 0:64] + first_sum[64:128, 64:128]
    packed = jnp.concatenate(
        [total, jnp.concatenate([corner[0:32], corner[32:64]], axis=1)], axis=0
    )
    for j in range(8):
        send[j, 96:108, :] = packed[12 * j : 12 * j + 12]


def sum_kernel(*refs):
    parts, latent_out, weights_out = refs
    total = parts[0]
    for j in range(1, 8):
        total = total + parts[j]
    for q in range(24):
        a, t = divmod(q, 4)
        for c in range(4):
            latent_out[c, a : a + 1, 128 * t : 128 * t + 128] = total[4 * q + c : 4 * q + c + 1]
    weights_out[...] = total[96:108]


def pack_kernel(press, vel, back_vel, low_x, high_x, low_y, high_y, sems):
    copies = []

    def copy(source, target):
        copies.append(pltpu.make_async_copy(source, target, sems.at[len(copies)]))

    copy(press.at[pl.ds(0, HP)], low_x.at[pl.ds(0, HP)])
    copy(press.at[pl.ds(NXT - HP, HP)], high_x.at[pl.ds(0, HP)])
    copy(press.at[:, pl.ds(0, 8)], low_y.at[:, pl.ds(0, 8)])
    copy(press.at[:, pl.ds(24, 8)], high_y.at[:, pl.ds(0, 8)])
    for place, field in ((0, vel), (1, back_vel)):
        layers, rows = pl.ds(HP + HV * place, HV), pl.ds(8 + 8 * place, 8)
        copy(field.at[0, pl.ds(0, HV)], low_x.at[layers])
        copy(field.at[0, pl.ds(NXT - HV, HV)], high_x.at[layers])
        copy(field.at[1, :, pl.ds(0, 8)], low_y.at[:, rows])
        copy(field.at[1, :, pl.ds(24, 8)], high_y.at[:, rows])
    for each in copies:
        each.start()
    for each in copies:
        each.wait()


def pack(press, vel, back_vel):
    beside_x, beside_y = shape(HP + 2 * HV, NYT, NZ), shape(NXT, 24, NZ)
    return pl.pallas_call(
        pack_kernel,
        out_shape=(beside_x, beside_x, beside_y, beside_y),
        in_specs=[pl.BlockSpec(memory_space=pl.ANY)] * 3,
        out_specs=(VMEM,) * 4,
        scratch_shapes=[pltpu.SemaphoreType.DMA((12,))],
        compiler_params=pltpu.CompilerParams(vmem_limit_bytes=8 * 1024 * 1024),
    )(press, vel, back_vel)


def final_kernel(parts, second_out, first_out):
    whole = jnp.concatenate([parts[j] for j in range(8)], axis=0)
    second_out[...] = whole[:64]
    first_out[0:32] = whole[64:, :64]
    first_out[32:64] = whole[64:, 64:]


def receiver_fields(rec_pos, observed, anchor_x, anchor_y):
    local_x = rec_pos[0] - anchor_x
    local_y = rec_pos[1] - anchor_y
    inside = (local_x >= 0) & (local_x < NXT) & (local_y >= 0) & (local_y < NYT)
    row = jnp.where(inside, local_x * NYT + local_y, -1)
    rows = (lax.broadcasted_iota(jnp.int32, (NXT * NYT, row.shape[0]), 0) == row).astype(
        jnp.bfloat16
    )
    coarse = lax.reduce_precision(observed, 8, 7)
    rest = observed - coarse
    values = jnp.concatenate([jnp.ones((1, row.shape[0]), F32), coarse, rest], axis=0)
    hit = lax.broadcasted_iota(jnp.int32, (row.shape[0], NZ), 1) == rec_pos[2][:, None]
    spread = jnp.where(hit[:, None, :], values.T[:, :, None], 0.0).astype(jnp.bfloat16)
    fields = jnp.dot(
        rows, spread.reshape(row.shape[0], 7 * NZ), preferred_element_type=F32
    ).reshape(NXT, NYT, 7, NZ)
    fields = fields.transpose(2, 0, 1, 3)
    return fields[0], fields[1:4] + fields[4:7]


def body(
    latent,
    w_first,
    w_second,
    fwd_press,
    fwd_vel,
    adj_press,
    adj_vel,
    src_pos,
    src_amp,
    rec_pos,
    observed,
):
    anchor_x, anchor_y = lax.axis_index("gx") * NXT, lax.axis_index("gy") * NYT
    scalars = (src_pos.reshape(3), src_amp.reshape(3))

    flat = latent.reshape(4, 24, 128).transpose(1, 0, 2).reshape(96, 128)
    blocks = lax.all_to_all(jnp.broadcast_to(flat, (8, 96, 128)), "shot", 0, 0, tiled=True)

    press, back_press = fwd_press[0], adj_press[0]
    vel, back_vel = fwd_vel[0], adj_vel[0]
    beside = exchange(*pack(press, vel, back_vel))
    count, obs = receiver_fields(rec_pos[0], observed[0], anchor_x, anchor_y)

    tile = shape(NXT, NYT, NZ)
    beside_x, beside_y = shape(HV, NYT, NZ), shape(NXT, 8, NZ)
    decoded = call(
        decode_kernel,
        [tile, tile, beside_x, beside_x, beside_y, beside_y, tile, tile]
        + [shape(GROUPS, 128, 2 * NZ)] * 2,
        0,
        [w_first, w_second, blocks],
    )
    modulus, buoyancy = decoded[:2]
    material = (buoyancy,) + exchange(*decoded[2:6]) + (modulus,)
    sig_speed, sig_dens, latent_wide, hidden_wide = decoded[6:]

    stored, earlier = [], []
    state_p = (press,) + beside
    state_v = (vel,) + beside
    offsets = (0, HP, 0, 8)
    for moment in range(STEPS):
        last = moment == STEPS - 1
        extra = [count, obs, back_press] if last else []
        outs = step(moment, True, last, offsets, scalars, state_p, state_v, material, extra)
        stored.append(outs[:2])
        outs = outs[2:]
        if not last:
            earlier.append(outs[0])
            state_v = outs[5:]
        state_p = (outs[0],) + exchange(*outs[1:5])
        offsets = (0, 0, 0, 0)
    state_v = (back_vel,) + beside
    offsets = (0, HP + HV, 0, 16)
    sums = []
    for moment in reversed(range(STEPS)):
        last = moment == 0
        extra = list(stored[moment]) + sums
        if not last:
            extra += [count, obs, earlier[moment - 1]]
        outs = step(moment, False, last, offsets, (), state_p, state_v, material, extra)
        sums = list(outs[:2])
        if not last:
            state_p = (outs[2],) + exchange(*outs[3:7])
            state_v = outs[7:]
        offsets = (0, 0, 0, 0)

    (send,) = call(
        grads_kernel,
        [shape(8, 108, 128)],
        0,
        [w_first, w_second] + sums
        + [sig_speed, sig_dens, latent_wide, hidden_wide],
        [pltpu.VMEM((128, 256), F32), pltpu.VMEM((128, 128), F32)],
    )
    parts = lax.all_to_all(send, "shot", 0, 0, tiled=True)
    grad_latent, weights = call(sum_kernel, [shape(4, 6, 512), shape(12, 128)], 0, [parts])
    group = lax.axis_size("gx") * lax.axis_size("gy")
    weights = lax.all_to_all(
        jnp.broadcast_to(weights, (group, 12, 128)), ("gx", "gy"), 0, 0, tiled=True
    )
    weights = jnp.sum(weights, axis=0)
    weights = lax.all_to_all(jnp.broadcast_to(weights, (8, 12, 128)), "shot", 0, 0, tiled=True)
    grad_second, grad_first = call(
        final_kernel, [shape(CH, 128), shape(CH, CH)], 0, [weights]
    )
    return (grad_latent, grad_first, grad_second)


def solution(mesh):
    in_specs = (
        P("shot", "gx", "gy"),
        P(),
        P(),
        P("shot", "gx", "gy", None),
        P("shot", None, "gx", "gy", None),
        P("shot", "gx", "gy", None),
        P("shot", None, "gx", "gy", None),
        P(None, "shot"),
        P(None, "shot"),
        P("shot", None, None),
        P("shot", None, None),
    )
    out_specs = (P("shot", "gx", "gy"), P(), P())
    return jax.shard_map(body, mesh=mesh, in_specs=in_specs, out_specs=out_specs, check_vma=False)
```

```python
import functools

import jax
import jax.numpy as jnp
from jax import lax
from jax.experimental import pallas as pl
from jax.experimental.pallas import tpu as pltpu
from jax.sharding import PartitionSpec as P

CH = 64
STEPS = 3
coeffs = (1225.0 / 1024.0, -245.0 / 3072.0, 49.0 / 5120.0, -5.0 / 7168.0)

NXT, NYT, NZ = 24, 32, 128
GROUPS = 12
HP = 7
HV = 4
HI = lax.Precision.HIGHEST
F32 = jnp.float32
BF16 = jnp.bfloat16
UNROLL = (8, 8, 8)
VMEM = pl.BlockSpec(memory_space=pltpu.VMEM)
SMEM = pl.BlockSpec(memory_space=pltpu.SMEM)


def shape(*dims):
    return jax.ShapeDtypeStruct(dims, F32)


def call(kernel, outs, smem_count, args, scratch=(), flops=10**7):
    nbytes = 4 * sum(a.size for a in args) + 4 * sum(o.size for o in outs)
    return pl.pallas_call(
        kernel,
        out_shape=tuple(outs),
        in_specs=[SMEM] * smem_count + [VMEM] * (len(args) - smem_count),
        out_specs=tuple(VMEM for _ in outs),
        scratch_shapes=list(scratch),
        compiler_params=pltpu.CompilerParams(vmem_limit_bytes=16 * 1024 * 1024),
        cost_estimate=pl.CostEstimate(flops=flops, bytes_accessed=nbytes, transcendentals=0),
    )(*args)


def ring(value, axis, shift):
    count = lax.axis_size(axis)
    return lax.ppermute(value, axis, [(i, (i + shift) % count) for i in range(count)])


def up_depth(value, shift, lane):
    if shift == 0:
        return value
    rolled = pltpu.roll(value, (-shift) % NZ, 1)
    keep = lane < NZ - shift if shift > 0 else lane >= -shift
    return jnp.where(keep, rolled, 0.0)


def plus(take):
    summed = coeffs[0] * (take(1) - take(0))
    for r in (2, 3, 4):
        summed = summed + coeffs[r - 1] * (take(r) - take(1 - r))
    return summed


def minus(take):
    summed = coeffs[0] * (take(0) - take(-1))
    for r in (2, 3, 4):
        summed = summed + coeffs[r - 1] * (take(r - 1) - take(-r))
    return summed


def step_kernel(moment, forward, last, off_p, off_v, row_p, row_v, *refs):
    refs = list(refs)
    take = refs.pop
    source, amps = (take(0), take(0)) if forward else (None, None)
    press, pxl, pxh, pyl, pyh = [take(0) for _ in range(5)]
    vel, vxl, vxh, vyl, vyh = [take(0) for _ in range(5)]
    buoy, bxl, bxh, byl, byh, modu = [take(0) for _ in range(6)]
    dz = take(0)
    count = obs = back = earlier = None
    if forward and last:
        count, obs, back = [take(0) for _ in range(3)]
    elif not forward and not last:
        count, obs, earlier = [take(0) for _ in range(3)]
    elif not forward:
        vz_in, div_in, slope_in, slope_z_in, gm_in, gb_in = [take(0) for _ in range(6)]
    if forward:
        div_out, slope_out = take(0), take(0)
    elif last:
        gm_out, gb_out = take(0), take(0)
    else:
        bare_out = take(0)
    ends = forward or not last
    if ends:
        p_out, sxl, sxh, syl, syh = [take(0) for _ in range(5)]
    if not last:
        vel_out, vxl_out, vxh_out, vyl_out, vyh_out = [take(0) for _ in range(5)]
    wide, vx, tall, vy_tall = [take(0) for _ in range(4)]

    at_x, at_y = lax.axis_index("gx"), lax.axis_index("gy")
    low_x = jnp.where(at_x > 0, 1.0, 0.0)
    high_x = jnp.where(at_x < lax.axis_size("gx") - 1, 1.0, 0.0)
    low_y = jnp.where(at_y > 0, 1.0, 0.0)
    high_y = jnp.where(at_y < lax.axis_size("gy") - 1, 1.0, 0.0)
    for i in range(HP):
        wide[i] = pxl[off_p + i] * low_x
        wide[HP + NXT + i] = pxh[off_p + i] * high_x

    nothing = jnp.zeros((8, NZ), F32)

    def copy(x, carry):
        here = press[x]
        wide[x + HP] = here
        tall[x, 0:8] = nothing
        tall[x, 8:16] = pyl[x, row_p : row_p + 8] * low_y
        tall[x, 16:48] = here
        tall[x, 48:56] = pyh[x, row_p : row_p + 8] * high_y
        tall[x, 56:64] = nothing
        vy_tall[x, 0:8] = nothing
        vy_tall[x, 56:64] = nothing
        return carry

    lax.fori_loop(0, NXT, copy, 0, unroll=UNROLL[0])

    def slope_x(i):
        return plus(lambda s: wide[i + 3 + s])

    for i in range(HV):
        vx[i] = low_x * (vxl[off_v + i] - bxl[i] * slope_x(i))
        if not last:
            vxl_out[i] = vx[i]
    for i in range(HV - 1):
        at = HV + NXT + i
        vx[at] = high_x * (vxh[off_v + i] - bxh[i] * slope_x(at))
        if not last:
            vxh_out[i] = vx[at]
    if not last:
        vxh_out[HV - 1] = jnp.zeros((NYT, NZ), F32)

    def first(x, carry):
        b_here = buoy[x]
        slope = slope_x(x + HV)
        new = vel[0, x] - b_here * slope
        vx[x + HV] = new
        slope_y = plus(lambda s: tall[x, 8 + s : 56 + s])
        vy_low = low_y * (vyl[x, row_v : row_v + 8] - byl[x] * slope_y[0:8])
        vy = vel[1, x] - b_here * slope_y[8:40]
        vy_high = high_y * (vyh[x, row_v : row_v + 8] - byh[x] * slope_y[40:48])
        vy_tall[x, 8:16] = vy_low
        vy_tall[x, 16:48] = vy
        vy_tall[x, 48:56] = vy_high
        if not last:
            vel_out[0, x] = new
            vel_out[1, x] = vy
            vyl_out[x] = vy_low
            vyh_out[x] = vy_high
        if forward:
            slope_out[0, x] = slope
            slope_out[1, x] = slope_y[8:40]
        return carry

    lax.fori_loop(0, NXT, first, 0, unroll=UNROLL[1])

    if forward:
        lane = lax.broadcasted_iota(jnp.int32, (NYT, NZ), 1)
        cell = lax.broadcasted_iota(jnp.int32, (NYT, NZ), 0) * NZ + lane
        source_x = source[0] - at_x * NXT
        source_y = source[1] - at_y * NYT
        source_at = jnp.where((source_y >= 0) & (source_y < NYT), source_y * NZ + source[2], -1)
        amplitude = amps[moment]

    def second(x, carry):
        here = press[x]
        diverge = minus(lambda s: vx[x + HV + s])
        diverge = diverge + minus(lambda s: vy_tall[x, 16 + s : 48 + s])
        diverge = diverge + dz[x]
        new = here - modu[x] * diverge
        if forward:
            div_out[x] = diverge
            at = jnp.where(x == source_x, source_at, -1)
            new = new + jnp.where(cell == at, amplitude, 0.0)
            if last:
                new = back[x] + (count[x] * new - obs[moment, x])
        elif last:
            gm_out[x] = gm_in[x] - new * div_in[x]
            gb_out[x] = gb_in[x] - (
                vx[x + HV] * slope_in[0, x]
                + vy_tall[x, 16:48] * slope_in[1, x]
                + vz_in[x] * slope_z_in[x]
            )
        else:
            bare_out[x] = new
            new = new + (count[x] * earlier[x] - obs[moment - 1, x])
        if ends:
            p_out[x] = new
            syl[x] = new[0:8]
            syh[x] = new[24:32]
        return carry

    lax.fori_loop(0, NXT, second, 0, unroll=UNROLL[2])
    if ends:
        for i in range(HP):
            sxl[i] = p_out[i]
            sxh[i] = p_out[NXT - HP + i]


def step(moment, forward, last, offsets, scalars, press, vel, material, extra):
    tile = shape(NXT, NYT, NZ)
    two = shape(2, NXT, NYT, NZ)
    beside_y = shape(NXT, 8, NZ)
    outs = [tile, two] if forward else [tile, tile] if last else [tile]
    if forward or not last:
        outs += [tile, shape(HP, NYT, NZ), shape(HP, NYT, NZ), beside_y, beside_y]
    if not last:
        outs += [two, shape(HV, NYT, NZ), shape(HV, NYT, NZ), beside_y, beside_y]
    args = list(scalars) + list(press) + list(vel) + list(material) + list(extra)
    scratch = [
        pltpu.VMEM(dims, F32)
        for dims in (
            (NXT + 2 * HP, NYT, NZ),
            (NXT + 2 * HV, NYT, NZ),
            (NXT, NYT + 32, NZ),
            (NXT, NYT + 32, NZ),
        )
    ]
    kernel = functools.partial(step_kernel, moment, forward, last, *offsets)
    return call(kernel, outs, len(scalars), args, scratch)


def depth_kernel(slopes, sums, *refs):
    refs = list(refs)
    take = refs.pop
    press, vz_in, buoy = [take(0) for _ in range(3)]
    if sums:
        bare, vel, div_in, slope_in, slope_z_in = [take(0) for _ in range(5)]
        gm_in, gb_in = (take(0), take(0)) if sums == 2 else (None, None)
    vz_out, dz_out = take(0), take(0)
    slope_out = take(0) if slopes else None
    if sums:
        gm_out, gb_out = take(0), take(0)
    lane = lax.broadcasted_iota(jnp.int32, (NYT, NZ), 1)

    def layer(x, carry):
        slope = plus(lambda s: up_depth(press[x], s, lane))
        old = vz_in[2, x] if len(vz_in.shape) == 4 else vz_in[x]
        vz = old - buoy[x] * slope
        vz_out[x] = vz
        dz_out[x] = minus(lambda s: up_depth(vz, s, lane))
        if slopes:
            slope_out[x] = slope
        if sums:
            part_m = -bare[x] * div_in[x]
            part_b = vel[0, x] * slope_in[0, x] + vel[1, x] * slope_in[1, x]
            part_b = -(part_b + old * slope_z_in[x])
            gm_out[x] = part_m if gm_in is None else gm_in[x] + part_m
            gb_out[x] = part_b if gb_in is None else gb_in[x] + part_b
        return carry

    lax.fori_loop(0, NXT, layer, 0, unroll=UNROLL[1])


def depth(slopes, press, vz, buoy, terms=(), sums=()):
    tile = shape(NXT, NYT, NZ)
    outs = [tile] * (2 + slopes + (2 if terms else 0))
    mode = 0 if not terms else 2 if sums else 1
    kernel = functools.partial(depth_kernel, slopes, mode)
    return call(kernel, outs, 0, [press, vz, buoy] + list(terms) + list(sums))


def exchange(low_x, high_x, low_y, high_y):
    return (
        ring(high_x, "gx", 1),
        ring(low_x, "gx", -1),
        ring(high_y, "gy", 1),
        ring(low_y, "gy", -1),
    )


def spread_rows():
    row = lax.broadcasted_iota(jnp.int32, (64, 2 * NZ), 0)
    lane = lax.broadcasted_iota(jnp.int32, (64, 2 * NZ), 1)
    same = ((row >> 2) & 1) == (lane >> 7)
    depth = (row >> 3) * 4 + (row & 3)
    return jnp.where(same & (((lane & 127) >> 2) == depth), 1.0, 0.0).astype(BF16)


def split(value):
    high = value.astype(BF16)
    return high, (value - high.astype(F32)).astype(BF16)


def dot(a, b, dims=((1,), (0,))):
    return lax.dot_general(a, b, (dims, ((), ())), preferred_element_type=F32)


def stack_right(value):
    high, low = split(value)
    return jnp.concatenate([high, high, low], axis=0)


def dot_rows(a, b):
    dims = ((1,), (1,))
    return dot(a[0], b[0], dims) + (dot(a[0], b[1], dims) + dot(a[1], b[0], dims))


def reorder():
    row = lax.broadcasted_iota(jnp.int32, (256, 128), 0)
    natural = (((row >> 3) & 7) << 4) + ((row & 3) << 2) + (row >> 6)
    picked = natural == lax.broadcasted_iota(jnp.int32, (256, 128), 1)
    return jnp.where(picked, 1.0, 0.0)


def two_blocks(matrix):
    empty = jnp.zeros((CH, CH), F32)
    return jnp.concatenate(
        [jnp.concatenate([matrix, empty], axis=1), jnp.concatenate([empty, matrix], axis=1)],
        axis=0,
    )


def stack_left(matrix):
    high, low = split(matrix)
    return jnp.concatenate([high, low, high], axis=1)


def phases(dtype):
    lane = lax.broadcasted_iota(jnp.int32, (64, 2 * NZ), 1) & 3
    return [jnp.where(lane == k, 1.0, 0.0).astype(dtype) for k in range(4)]


def decode_kernel(w_first, w_second, blocks, *refs):
    modu, buoy, bxl, bxh, byl, byh, sig_speed, sig_dens, latent_out, hidden_out = refs
    spread = spread_rows()
    spread = jnp.concatenate([spread, spread, spread], axis=0)
    phase = lax.broadcasted_iota(jnp.int32, (64, 2 * NZ), 1) & 3
    mix_first = stack_left(two_blocks(w_first[...]).T)
    chosen = reorder().astype(BF16)
    cell = (lax.broadcasted_iota(jnp.int32, (256, CH), 0) >> 2) & 1
    pieces = []
    for piece in split(w_second[...]):
        rows = dot(chosen, piece, ((1,), (1,)))
        pieces.append(
            jnp.concatenate([jnp.where(cell == b, rows, 0.0) for b in range(2)], axis=1)
        )
    pieces = [piece.astype(BF16) for piece in pieces]
    mix_second = jnp.concatenate([pieces[0], pieces[1], pieces[0]], axis=1)
    for g in range(GROUPS):
        a, half = divmod(g, 2)
        rows = blocks[:, 8 * g : 8 * g + 8, :].reshape(64, 128)
        high, rest = rows.astype(BF16), None
        rest = rows - high.astype(F32)
        middle, low = split(rest)
        pieces = jnp.concatenate([high, middle, low], axis=0)
        latent = dot(pieces, spread, ((0,), (0,)))
        hidden = jnp.tanh(dot(mix_first, stack_right(latent)))
        latent_out[g] = latent
        hidden_out[g] = hidden
        out = dot(mix_second, stack_right(hidden))
        fine = out[0:64]
        for k in (1, 2, 3):
            fine = jnp.where(phase == k, out[64 * k : 64 * k + 64], fine)
        sig = jax.nn.sigmoid(fine)
        s1, s2 = sig[0:32], sig[32:64]
        speed = 0.15 + 0.25 * s1
        dens = 1.0 + 1.5 * s2
        mod = dens * speed * speed
        inv = 1.0 / dens
        for i in range(4):
            for q in range(2):
                x = 4 * a + i
                ys = slice(16 * half + 8 * q, 16 * half + 8 * q + 8)
                part = (slice(8 * i, 8 * i + 8), slice(NZ * q, NZ * q + NZ))
                sig_speed[x, ys] = s1[part]
                sig_dens[x, ys] = s2[part]
                modu[x, ys] = mod[part]
                buoy[x, ys] = inv[part]
    for i in range(HV):
        bxl[i] = buoy[i]
        bxh[i] = buoy[NXT - HV + i]
    byl[...] = buoy[:, 0:8, :]
    byh[...] = buoy[:, 24:32, :]


def grads_kernel(
    w_first, w_second, gm, gb, sig_speed, sig_dens, latent_in, hidden_in, *refs
):
    send, second_sum, first_sum = refs
    spread = spread_rows()
    spread = jnp.concatenate([spread, spread], axis=1)
    masks = phases(BF16)
    back_first = stack_left(two_blocks(w_first[...]))
    order = reorder()
    chosen = order.astype(BF16)
    cell = (lax.broadcasted_iota(jnp.int32, (CH, 256), 1) >> 2) & 1
    pieces = []
    for piece in split(w_second[...]):
        columns = dot(piece, chosen, ((1,), (1,)))
        pieces.append(
            jnp.concatenate([jnp.where(cell == b, columns, 0.0) for b in range(2)], axis=0)
        )
    pieces = [piece.astype(BF16) for piece in pieces]
    back_second = jnp.concatenate([pieces[0], pieces[1], pieces[0]], axis=1)

    def square(field, a, half):
        return jnp.concatenate(
            [
                jnp.concatenate(
                    [field[4 * a + i, 16 * half + 8 * q : 16 * half + 8 * q + 8] for i in range(4)],
                    axis=0,
                )
                for q in range(2)
            ],
            axis=1,
        )

    for g in range(GROUPS):
        a, half = divmod(g, 2)
        s1, s2 = square(sig_speed, a, half), square(sig_dens, a, half)
        g_mod, g_buoy = square(gm, a, half), square(gb, a, half)
        speed = 0.15 + 0.25 * s1
        dens = 1.0 + 1.5 * s2
        grad_speed = g_mod * 2.0 * dens * speed
        grad_dens = g_mod * speed * speed - g_buoy / (dens * dens)
        fine = jnp.concatenate(
            [grad_speed * 0.25 * s1 * (1.0 - s1), grad_dens * 1.5 * s2 * (1.0 - s2)], axis=0
        )
        high, low = split(fine)
        high = jnp.concatenate([high * mask for mask in masks], axis=0)
        low = jnp.concatenate([low * mask for mask in masks], axis=0)
        latent, hidden = latent_in[g], hidden_in[g]
        grad_hidden = dot(back_second, jnp.concatenate([high, high, low], axis=0))
        grad_pre = grad_hidden * (1.0 - hidden * hidden)
        pre = split(grad_pre)
        grad_latent = dot(back_first, jnp.concatenate([pre[0], pre[0], pre[1]], axis=0))
        gathered = dot(
            spread, jnp.concatenate(split(grad_latent), axis=1), ((1,), (1,))
        )
        for j in range(8):
            send[j, 8 * g : 8 * g + 8, :] = gathered[8 * j : 8 * j + 8]
        second = dot_rows(split(hidden), (high, low))
        first = dot_rows(split(latent), pre)
        if g == 0:
            second_sum[...] = second
            first_sum[...] = first
        else:
            second_sum[...] += second
            first_sum[...] += first
    column = lax.broadcasted_iota(jnp.int32, (CH, 256), 1)
    total = jnp.where(((column >> 2) & 1) == 0, second_sum[0:64], second_sum[64:128])
    total = lax.dot_general(
        total, order, (((1,), (0,)), ((), ())), precision=HI, preferred_element_type=F32
    )
    corner = first_sum[0:64, 0:64] + first_sum[64:128, 64:128]
    packed = jnp.concatenate(
        [total, jnp.concatenate([corner[0:32], corner[32:64]], axis=1)], axis=0
    )
    for j in range(8):
        send[j, 96:108, :] = packed[12 * j : 12 * j + 12]


def sum_kernel(*refs):
    parts, latent_out, weights_out = refs
    total = parts[0]
    for j in range(1, 8):
        total = total + parts[j]
    for q in range(24):
        a, t = divmod(q, 4)
        for c in range(4):
            latent_out[c, a : a + 1, 128 * t : 128 * t + 128] = total[4 * q + c : 4 * q + c + 1]
    weights_out[...] = total[96:108]


def pack_kernel(press, vel, back_vel, low_x, high_x, low_y, high_y, sems):
    copies = []

    def copy(source, target):
        copies.append(pltpu.make_async_copy(source, target, sems.at[len(copies)]))

    copy(press.at[pl.ds(0, HP)], low_x.at[pl.ds(0, HP)])
    copy(press.at[pl.ds(NXT - HP, HP)], high_x.at[pl.ds(0, HP)])
    copy(press.at[:, pl.ds(0, 8)], low_y.at[:, pl.ds(0, 8)])
    copy(press.at[:, pl.ds(24, 8)], high_y.at[:, pl.ds(0, 8)])
    for place, field in ((0, vel), (1, back_vel)):
        layers, rows = pl.ds(HP + HV * place, HV), pl.ds(8 + 8 * place, 8)
        copy(field.at[0, pl.ds(0, HV)], low_x.at[layers])
        copy(field.at[0, pl.ds(NXT - HV, HV)], high_x.at[layers])
        copy(field.at[1, :, pl.ds(0, 8)], low_y.at[:, rows])
        copy(field.at[1, :, pl.ds(24, 8)], high_y.at[:, rows])
    for each in copies:
        each.start()
    for each in copies:
        each.wait()


def pack(press, vel, back_vel):
    beside_x, beside_y = shape(HP + 2 * HV, NYT, NZ), shape(NXT, 24, NZ)
    return pl.pallas_call(
        pack_kernel,
        out_shape=(beside_x, beside_x, beside_y, beside_y),
        in_specs=[pl.BlockSpec(memory_space=pl.ANY)] * 3,
        out_specs=(VMEM,) * 4,
        scratch_shapes=[pltpu.SemaphoreType.DMA((12,))],
        compiler_params=pltpu.CompilerParams(vmem_limit_bytes=8 * 1024 * 1024),
    )(press, vel, back_vel)


def final_kernel(parts, second_out, first_out):
    whole = jnp.concatenate([parts[j] for j in range(8)], axis=0)
    second_out[...] = whole[:64]
    first_out[0:32] = whole[64:, :64]
    first_out[32:64] = whole[64:, 64:]


def receiver_kernel(pos, observed, after, count_out, obs_out, rows, spread):
    number = pos.shape[1]
    local_x = pos[0:1, :] - lax.axis_index("gx") * NXT
    local_y = pos[1:2, :] - lax.axis_index("gy") * NYT
    inside = (local_x >= 0) & (local_x < NXT) & (local_y >= 0) & (local_y < NYT)
    cell = jnp.where(inside, local_x * NYT + local_y, -1)
    depth_at = pos[2:3, :]
    high = [observed[n : n + 1, :].astype(BF16).astype(F32) for n in range(STEPS)]
    low = [observed[n : n + 1, :] - high[n] for n in range(STEPS)]
    values = [jnp.ones((1, number), F32)] + high + low
    row = lax.broadcasted_iota(jnp.int32, (NYT, number), 0)
    level = lax.broadcasted_iota(jnp.int32, (16, number), 0)

    def fill_rows(x, carry):
        rows[pl.ds(x * NYT, NYT), :] = jnp.where(row == cell - x * NYT, 1.0, 0.0).astype(BF16)
        return carry

    lax.fori_loop(0, NXT, fill_rows, 0)
    for k in range(NZ // 16):
        hit = level + 16 * k == depth_at
        for v, value in enumerate(values):
            spread[NZ * v + 16 * k : NZ * v + 16 * k + 16, :] = jnp.where(hit, value, 0.0).astype(
                BF16
            )

    def multiply(block, carry):
        out = dot(rows[pl.ds(block * 256, 256), :], spread[...], ((1,), (1,)))
        xs = pl.ds(block * 8, 8)
        count_out[xs] = out[:, 0:NZ].reshape(8, NYT, NZ)
        for n in range(STEPS):
            first = out[:, NZ * (1 + n) : NZ * (2 + n)]
            second = out[:, NZ * (4 + n) : NZ * (5 + n)]
            obs_out[n, xs] = (first + second).reshape(8, NYT, NZ)
        return carry

    lax.fori_loop(0, 3, multiply, 0)


def body(
    latent,
    w_first,
    w_second,
    fwd_press,
    fwd_vel,
    adj_press,
    adj_vel,
    src_pos,
    src_amp,
    rec_pos,
    observed,
):
    scalars = (src_pos.reshape(3), src_amp.reshape(3))

    flat = latent.reshape(4, 24, 128).transpose(1, 0, 2).reshape(96, 128)
    blocks = lax.all_to_all(jnp.broadcast_to(flat, (8, 96, 128)), "shot", 0, 0, tiled=True)

    press, back_press = fwd_press[0], adj_press[0]
    vel, back_vel = fwd_vel[0], adj_vel[0]
    beside = exchange(*pack(press, vel, back_vel))

    tile = shape(NXT, NYT, NZ)
    beside_x, beside_y = shape(HV, NYT, NZ), shape(NXT, 8, NZ)
    decoded = call(
        decode_kernel,
        [tile, tile, beside_x, beside_x, beside_y, beside_y, tile, tile]
        + [shape(GROUPS, 128, 2 * NZ)] * 2,
        0,
        [w_first, w_second, blocks],
    )
    modulus, buoyancy = decoded[:2]
    material = (buoyancy,) + exchange(*decoded[2:6]) + (modulus,)
    sig_speed, sig_dens, latent_wide, hidden_wide = decoded[6:]

    count, obs = call(
        receiver_kernel,
        [tile, shape(STEPS, NXT, NYT, NZ)],
        0,
        [rec_pos[0], observed[0], decoded[2]],
        [pltpu.VMEM((NXT * NYT, 2048), BF16), pltpu.VMEM((7 * NZ, 2048), BF16)],
        flops=3 * 10**9,
    )
    stored, earlier = [], []
    state_p = (press,) + beside
    state_v = (vel,) + beside
    vz = vel
    offsets = (0, HP, 0, 8)
    for moment in range(STEPS):
        last = moment == STEPS - 1
        vz, dz, slope_z = depth(True, state_p[0], vz, buoyancy)
        extra = [dz] + ([count, obs, back_press] if last else [])
        outs = step(moment, True, last, offsets, scalars, state_p, state_v, material, extra)
        stored.append(list(outs[:2]) + [slope_z])
        outs = outs[2:]
        if not last:
            earlier.append(outs[0])
            state_v = outs[5:]
        state_p = (outs[0],) + exchange(*outs[1:5])
        offsets = (0, 0, 0, 0)
    state_v = (back_vel,) + beside
    vz = back_vel
    offsets = (0, HP + HV, 0, 16)
    terms, sums = [], []
    for moment in reversed(range(STEPS)):
        last = moment == 0
        done = depth(False, state_p[0], vz, buoyancy, terms, sums)
        vz, dz, sums = done[0], done[1], list(done[2:])
        if last:
            extra = [dz, vz] + stored[moment] + sums
        else:
            extra = [dz, count, obs, earlier[moment - 1]]
        outs = step(moment, False, last, offsets, (), state_p, state_v, material, extra)
        if last:
            sums = list(outs)
        else:
            state_p = (outs[1],) + exchange(*outs[2:6])
            state_v = outs[6:]
            terms = [outs[0], state_v[0]] + stored[moment]
        offsets = (0, 0, 0, 0)

    (send,) = call(
        grads_kernel,
        [shape(8, 108, 128)],
        0,
        [w_first, w_second] + sums
        + [sig_speed, sig_dens, latent_wide, hidden_wide],
        [pltpu.VMEM((128, 256), F32), pltpu.VMEM((128, 128), F32)],
    )
    parts = lax.all_to_all(send, "shot", 0, 0, tiled=True)
    grad_latent, weights = call(sum_kernel, [shape(4, 6, 512), shape(12, 128)], 0, [parts])
    group = lax.axis_size("gx") * lax.axis_size("gy")
    weights = lax.all_to_all(
        jnp.broadcast_to(weights, (group, 12, 128)), ("gx", "gy"), 0, 0, tiled=True
    )
    weights = jnp.sum(weights, axis=0)
    weights = lax.all_to_all(jnp.broadcast_to(weights, (8, 12, 128)), "shot", 0, 0, tiled=True)
    grad_second, grad_first = call(
        final_kernel, [shape(CH, 128), shape(CH, CH)], 0, [weights]
    )
    return (grad_latent, grad_first, grad_second)


def solution(mesh):
    in_specs = (
        P("shot", "gx", "gy"),
        P(),
        P(),
        P("shot", "gx", "gy", None),
        P("shot", None, "gx", "gy", None),
        P("shot", "gx", "gy", None),
        P("shot", None, "gx", "gy", None),
        P(None, "shot"),
        P(None, "shot"),
        P("shot", None, None),
        P("shot", None, None),
    )
    out_specs = (P("shot", "gx", "gy"), P(), P())
    return jax.shard_map(body, mesh=mesh, in_specs=in_specs, out_specs=out_specs, check_vma=False)
```

```python
import functools

import jax
import jax.numpy as jnp
from jax import lax
from jax.experimental import pallas as pl
from jax.experimental.pallas import tpu as pltpu
from jax.sharding import PartitionSpec as P

CH = 64
STEPS = 3
coeffs = (1225.0 / 1024.0, -245.0 / 3072.0, 49.0 / 5120.0, -5.0 / 7168.0)

NXT, NYT, NZ = 24, 32, 128
GROUPS = 12
HP = 7
HV = 4
HI = lax.Precision.HIGHEST
F32 = jnp.float32
BF16 = jnp.bfloat16
UNROLL = (8, 8, 8)
VMEM = pl.BlockSpec(memory_space=pltpu.VMEM)
SMEM = pl.BlockSpec(memory_space=pltpu.SMEM)


def shape(*dims):
    return jax.ShapeDtypeStruct(dims, F32)


def call(kernel, outs, smem_count, args, scratch=(), flops=10**7):
    nbytes = 4 * sum(a.size for a in args) + 4 * sum(o.size for o in outs)
    return pl.pallas_call(
        kernel,
        out_shape=tuple(outs),
        in_specs=[SMEM] * smem_count + [VMEM] * (len(args) - smem_count),
        out_specs=tuple(VMEM for _ in outs),
        scratch_shapes=list(scratch),
        compiler_params=pltpu.CompilerParams(vmem_limit_bytes=16 * 1024 * 1024),
        cost_estimate=pl.CostEstimate(flops=flops, bytes_accessed=nbytes, transcendentals=0),
    )(*args)


def ring(value, axis, shift):
    count = lax.axis_size(axis)
    return lax.ppermute(value, axis, [(i, (i + shift) % count) for i in range(count)])


def plus(take):
    summed = coeffs[0] * (take(1) - take(0))
    for r in (2, 3, 4):
        summed = summed + coeffs[r - 1] * (take(r) - take(1 - r))
    return summed


def minus(take):
    summed = coeffs[0] * (take(0) - take(-1))
    for r in (2, 3, 4):
        summed = summed + coeffs[r - 1] * (take(r - 1) - take(-r))
    return summed


def step_kernel(moment, forward, last, off_p, off_v, row_p, row_v, *refs):
    refs = list(refs)
    take = refs.pop
    source, amps = (take(0), take(0)) if forward else (None, None)
    press, pxl, pxh, pyl, pyh = [take(0) for _ in range(5)]
    vel, vxl, vxh, vyl, vyh = [take(0) for _ in range(5)]
    buoy, bxl, bxh, byl, byh, modu = [take(0) for _ in range(6)]
    dz = take(0)
    riders = [take(0) for _ in range(2)] if forward and moment == 0 else []
    if forward and moment == 1:
        take(0)
    count = obs = back = earlier = None
    if forward and last:
        count, obs, back = [take(0) for _ in range(3)]
    elif not forward and not last:
        count, obs, earlier = [take(0) for _ in range(3)]
    elif not forward:
        vz_in, div_in, slope_in, slope_z_in, gm_in, gb_in = [take(0) for _ in range(6)]
    if forward:
        div_out, slope_out = take(0), take(0)
    elif last:
        gm_out, gb_out = take(0), take(0)
    else:
        bare_out = take(0)
    ends = forward or not last
    if ends:
        p_out, sxl, sxh, syl, syh = [take(0) for _ in range(5)]
    if not last:
        vel_out, vxl_out, vxh_out, vyl_out, vyh_out = [take(0) for _ in range(5)]
    wide, vx, tall, vy_tall = [take(0) for _ in range(4)]

    at_x, at_y = lax.axis_index("gx"), lax.axis_index("gy")
    low_x = jnp.where(at_x > 0, 1.0, 0.0)
    high_x = jnp.where(at_x < lax.axis_size("gx") - 1, 1.0, 0.0)
    low_y = jnp.where(at_y > 0, 1.0, 0.0)
    high_y = jnp.where(at_y < lax.axis_size("gy") - 1, 1.0, 0.0)
    for i in range(HP):
        wide[i] = pxl[off_p + i] * low_x
        wide[HP + NXT + i] = pxh[off_p + i] * high_x

    nothing = jnp.zeros((8, NZ), F32)

    def copy(x, carry):
        here = press[x]
        wide[x + HP] = here
        tall[x, 0:8] = nothing
        tall[x, 8:16] = pyl[x, row_p : row_p + 8] * low_y
        tall[x, 16:48] = here
        tall[x, 48:56] = pyh[x, row_p : row_p + 8] * high_y
        tall[x, 56:64] = nothing
        vy_tall[x, 0:8] = nothing
        vy_tall[x, 56:64] = nothing
        return carry

    lax.fori_loop(0, NXT, copy, 0, unroll=UNROLL[0])

    def slope_x(i):
        return plus(lambda s: wide[i + 3 + s])

    for i in range(HV):
        vx[i] = low_x * (vxl[off_v + i] - bxl[i] * slope_x(i))
        if not last:
            vxl_out[i] = vx[i]
    for i in range(HV - 1):
        at = HV + NXT + i
        vx[at] = high_x * (vxh[off_v + i] - bxh[i] * slope_x(at))
        if not last:
            vxh_out[i] = vx[at]
    if not last:
        vxh_out[HV - 1] = jnp.zeros((NYT, NZ), F32)

    def first(x, carry):
        b_here = buoy[x]
        slope = slope_x(x + HV)
        new = vel[0, x] - b_here * slope
        vx[x + HV] = new
        slope_y = plus(lambda s: tall[x, 8 + s : 56 + s])
        vy_low = low_y * (vyl[x, row_v : row_v + 8] - byl[x] * slope_y[0:8])
        vy = vel[1, x] - b_here * slope_y[8:40]
        vy_high = high_y * (vyh[x, row_v : row_v + 8] - byh[x] * slope_y[40:48])
        vy_tall[x, 8:16] = vy_low
        vy_tall[x, 16:48] = vy
        vy_tall[x, 48:56] = vy_high
        if not last:
            vel_out[0, x] = new
            vel_out[1, x] = vy
            vyl_out[x] = vy_low
            vyh_out[x] = vy_high
        if forward:
            slope_out[0, x] = slope
            slope_out[1, x] = slope_y[8:40]
        return carry

    lax.fori_loop(0, NXT, first, 0, unroll=UNROLL[1])

    if forward:
        lane = lax.broadcasted_iota(jnp.int32, (NYT, NZ), 1)
        cell = lax.broadcasted_iota(jnp.int32, (NYT, NZ), 0) * NZ + lane
        source_x = source[0] - at_x * NXT
        source_y = source[1] - at_y * NYT
        source_at = jnp.where((source_y >= 0) & (source_y < NYT), source_y * NZ + source[2], -1)
        amplitude = amps[moment]

    def second(x, carry):
        here = press[x]
        diverge = minus(lambda s: vx[x + HV + s])
        diverge = diverge + minus(lambda s: vy_tall[x, 16 + s : 48 + s])
        diverge = diverge + dz[x]
        new = here - modu[x] * diverge
        if forward:
            div_out[x] = diverge
            at = jnp.where(x == source_x, source_at, -1)
            new = new + jnp.where(cell == at, amplitude, 0.0)
            if last:
                new = back[x] + (count[x] * new - obs[moment, x])
        elif last:
            gm_out[x] = gm_in[x] - new * div_in[x]
            gb_out[x] = gb_in[x] - (
                vx[x + HV] * slope_in[0, x]
                + vy_tall[x, 16:48] * slope_in[1, x]
                + vz_in[x] * slope_z_in[x]
            )
        else:
            bare_out[x] = new
            new = new + (count[x] * earlier[x] - obs[moment - 1, x])
        if ends:
            p_out[x] = new
            syl[x] = new[0:8]
            syh[x] = new[24:32]
        return carry

    lax.fori_loop(0, NXT, second, 0, unroll=UNROLL[2])
    if ends:
        for i in range(HP):
            sxl[i] = p_out[i]
            sxh[i] = p_out[NXT - HP + i]
        for i in range(HV if riders else 0):
            sxl[HP + i] = riders[0][i]
            sxh[HP + i] = riders[1][i]


def step(moment, forward, last, offsets, scalars, press, vel, material, extra):
    tile = shape(NXT, NYT, NZ)
    two = shape(2, NXT, NYT, NZ)
    beside_y = shape(NXT, 8, NZ)
    outs = [tile, two] if forward else [tile, tile] if last else [tile]
    if forward or not last:
        send_x = shape(HP + (HV if forward and moment == 0 else 0), NYT, NZ)
        outs += [tile, send_x, send_x, beside_y, beside_y]
    if not last:
        outs += [two, shape(HV, NYT, NZ), shape(HV, NYT, NZ), beside_y, beside_y]
    args = list(scalars) + list(press) + list(vel) + list(material) + list(extra)
    scratch = [
        pltpu.VMEM(dims, F32)
        for dims in (
            (NXT + 2 * HP, NYT, NZ),
            (NXT + 2 * HV, NYT, NZ),
            (NXT, NYT + 32, NZ),
            (NXT, NYT + 32, NZ),
        )
    ]
    kernel = functools.partial(step_kernel, moment, forward, last, *offsets)
    return call(kernel, outs, len(scalars), args, scratch)


def pieces_of(value):
    high = value.astype(BF16)
    rest = value - high.astype(F32)
    middle = rest.astype(BF16)
    return high, middle, (rest - middle.astype(F32)).astype(BF16)


def band(ahead):
    row = lax.broadcasted_iota(jnp.int32, (NZ, NZ), 0)
    offset = row - lax.broadcasted_iota(jnp.int32, (NZ, NZ), 1) - ahead
    matrix = jnp.zeros((NZ, NZ), F32)
    for r in range(4):
        matrix = jnp.where(offset == r, coeffs[r], matrix)
        matrix = jnp.where(offset == -1 - r, -coeffs[r], matrix)
    high, middle, low = pieces_of(matrix)
    return jnp.concatenate([high, middle, low, high, middle, high], axis=0)


def along_depth(value, right):
    high, middle, low = pieces_of(value.reshape(-1, NZ))
    left = jnp.concatenate([high, high, high, middle, middle, low], axis=1)
    return dot(left, right).reshape(value.shape)


def depth_kernel(slopes, sums, *refs):
    refs = list(refs)
    take = refs.pop
    press, vz_in, buoy = [take(0) for _ in range(3)]
    if sums:
        bare, vel, div_in, slope_in, slope_z_in = [take(0) for _ in range(5)]
        gm_in, gb_in = (take(0), take(0)) if sums == 2 else (None, None)
    vz_out, dz_out = take(0), take(0)
    slope_out = take(0) if slopes else None
    if sums:
        gm_out, gb_out = take(0), take(0)
    right_plus, right_minus = band(1), band(0)

    def layers(block, carry):
        xs = pl.ds(block * 8, 8)
        slope = along_depth(press[xs], right_plus)
        old = vz_in[2, xs] if len(vz_in.shape) == 4 else vz_in[xs]
        vz = old - buoy[xs] * slope
        vz_out[xs] = vz
        dz_out[xs] = along_depth(vz, right_minus)
        if slopes:
            slope_out[xs] = slope
        if sums:
            part_m = -bare[xs] * div_in[xs]
            part_b = vel[0, xs] * slope_in[0, xs] + vel[1, xs] * slope_in[1, xs]
            part_b = -(part_b + old * slope_z_in[xs])
            gm_out[xs] = part_m if gm_in is None else gm_in[xs] + part_m
            gb_out[xs] = part_b if gb_in is None else gb_in[xs] + part_b
        return carry

    lax.fori_loop(0, NXT // 8, layers, 0, unroll=True)


def depth(slopes, press, vz, buoy, terms=(), sums=()):
    tile = shape(NXT, NYT, NZ)
    outs = [tile] * (2 + slopes + (2 if terms else 0))
    mode = 0 if not terms else 2 if sums else 1
    kernel = functools.partial(depth_kernel, slopes, mode)
    return call(kernel, outs, 0, [press, vz, buoy] + list(terms) + list(sums))


def exchange(low_x, high_x, low_y, high_y):
    return (
        ring(high_x, "gx", 1),
        ring(low_x, "gx", -1),
        ring(high_y, "gy", 1),
        ring(low_y, "gy", -1),
    )


def spread_rows():
    row = lax.broadcasted_iota(jnp.int32, (64, 2 * NZ), 0)
    lane = lax.broadcasted_iota(jnp.int32, (64, 2 * NZ), 1)
    same = ((row >> 2) & 1) == (lane >> 7)
    depth = (row >> 3) * 4 + (row & 3)
    return jnp.where(same & (((lane & 127) >> 2) == depth), 1.0, 0.0).astype(BF16)


def split(value):
    high = value.astype(BF16)
    return high, (value - high.astype(F32)).astype(BF16)


def dot(a, b, dims=((1,), (0,))):
    return lax.dot_general(a, b, (dims, ((), ())), preferred_element_type=F32)


def stack_right(value):
    high, low = split(value)
    return jnp.concatenate([high, high, low], axis=0)


def dot_rows(a, b):
    dims = ((1,), (1,))
    return dot(a[0], b[0], dims) + (dot(a[0], b[1], dims) + dot(a[1], b[0], dims))


def reorder():
    row = lax.broadcasted_iota(jnp.int32, (256, 128), 0)
    natural = (((row >> 3) & 7) << 4) + ((row & 3) << 2) + (row >> 6)
    picked = natural == lax.broadcasted_iota(jnp.int32, (256, 128), 1)
    return jnp.where(picked, 1.0, 0.0)


def two_blocks(matrix):
    empty = jnp.zeros((CH, CH), F32)
    return jnp.concatenate(
        [jnp.concatenate([matrix, empty], axis=1), jnp.concatenate([empty, matrix], axis=1)],
        axis=0,
    )


def stack_left(matrix):
    high, low = split(matrix)
    return jnp.concatenate([high, low, high], axis=1)


def phases(dtype):
    lane = lax.broadcasted_iota(jnp.int32, (64, 2 * NZ), 1) & 3
    return [jnp.where(lane == k, 1.0, 0.0).astype(dtype) for k in range(4)]


def decode_kernel(w_first, w_second, blocks, *refs):
    modu, buoy, bxl, bxh, byl, byh, sig_speed, sig_dens, latent_out, hidden_out = refs
    spread = spread_rows()
    spread = jnp.concatenate([spread, spread, spread], axis=0)
    phase = lax.broadcasted_iota(jnp.int32, (64, 2 * NZ), 1) & 3
    mix_first = stack_left(two_blocks(w_first[...]).T)
    chosen = reorder().astype(BF16)
    cell = (lax.broadcasted_iota(jnp.int32, (256, CH), 0) >> 2) & 1
    pieces = []
    for piece in split(w_second[...]):
        rows = dot(chosen, piece, ((1,), (1,)))
        pieces.append(
            jnp.concatenate([jnp.where(cell == b, rows, 0.0) for b in range(2)], axis=1)
        )
    pieces = [piece.astype(BF16) for piece in pieces]
    mix_second = jnp.concatenate([pieces[0], pieces[1], pieces[0]], axis=1)
    for g in range(GROUPS):
        a, half = divmod(g, 2)
        rows = blocks[:, 8 * g : 8 * g + 8, :].reshape(64, 128)
        high, rest = rows.astype(BF16), None
        rest = rows - high.astype(F32)
        middle, low = split(rest)
        pieces = jnp.concatenate([high, middle, low], axis=0)
        latent = dot(pieces, spread, ((0,), (0,)))
        hidden = jnp.tanh(dot(mix_first, stack_right(latent)))
        latent_out[g] = latent
        hidden_out[g] = hidden
        out = dot(mix_second, stack_right(hidden))
        fine = out[0:64]
        for k in (1, 2, 3):
            fine = jnp.where(phase == k, out[64 * k : 64 * k + 64], fine)
        sig = jax.nn.sigmoid(fine)
        s1, s2 = sig[0:32], sig[32:64]
        speed = 0.15 + 0.25 * s1
        dens = 1.0 + 1.5 * s2
        mod = dens * speed * speed
        inv = 1.0 / dens
        for i in range(4):
            for q in range(2):
                x = 4 * a + i
                ys = slice(16 * half + 8 * q, 16 * half + 8 * q + 8)
                part = (slice(8 * i, 8 * i + 8), slice(NZ * q, NZ * q + NZ))
                sig_speed[x, ys] = s1[part]
                sig_dens[x, ys] = s2[part]
                modu[x, ys] = mod[part]
                buoy[x, ys] = inv[part]
    for i in range(HV):
        bxl[i] = buoy[i]
        bxh[i] = buoy[NXT - HV + i]
    byl[...] = buoy[:, 0:8, :]
    byh[...] = buoy[:, 24:32, :]


def grads_kernel(
    w_first, w_second, gm, gb, sig_speed, sig_dens, latent_in, hidden_in, *refs
):
    send, second_sum, first_sum = refs
    spread = spread_rows()
    spread = jnp.concatenate([spread, spread], axis=1)
    masks = phases(BF16)
    back_first = stack_left(two_blocks(w_first[...]))
    order = reorder()
    chosen = order.astype(BF16)
    cell = (lax.broadcasted_iota(jnp.int32, (CH, 256), 1) >> 2) & 1
    pieces = []
    for piece in split(w_second[...]):
        columns = dot(piece, chosen, ((1,), (1,)))
        pieces.append(
            jnp.concatenate([jnp.where(cell == b, columns, 0.0) for b in range(2)], axis=0)
        )
    pieces = [piece.astype(BF16) for piece in pieces]
    back_second = jnp.concatenate([pieces[0], pieces[1], pieces[0]], axis=1)

    def square(field, a, half):
        return jnp.concatenate(
            [
                jnp.concatenate(
                    [field[4 * a + i, 16 * half + 8 * q : 16 * half + 8 * q + 8] for i in range(4)],
                    axis=0,
                )
                for q in range(2)
            ],
            axis=1,
        )

    for g in range(GROUPS):
        a, half = divmod(g, 2)
        s1, s2 = square(sig_speed, a, half), square(sig_dens, a, half)
        g_mod, g_buoy = square(gm, a, half), square(gb, a, half)
        speed = 0.15 + 0.25 * s1
        dens = 1.0 + 1.5 * s2
        grad_speed = g_mod * 2.0 * dens * speed
        grad_dens = g_mod * speed * speed - g_buoy / (dens * dens)
        fine = jnp.concatenate(
            [grad_speed * 0.25 * s1 * (1.0 - s1), grad_dens * 1.5 * s2 * (1.0 - s2)], axis=0
        )
        high, low = split(fine)
        high = jnp.concatenate([high * mask for mask in masks], axis=0)
        low = jnp.concatenate([low * mask for mask in masks], axis=0)
        latent, hidden = latent_in[g], hidden_in[g]
        grad_hidden = dot(back_second, jnp.concatenate([high, high, low], axis=0))
        grad_pre = grad_hidden * (1.0 - hidden * hidden)
        pre = split(grad_pre)
        grad_latent = dot(back_first, jnp.concatenate([pre[0], pre[0], pre[1]], axis=0))
        gathered = dot(
            spread, jnp.concatenate(split(grad_latent), axis=1), ((1,), (1,))
        )
        for j in range(8):
            send[j, 8 * g : 8 * g + 8, :] = gathered[8 * j : 8 * j + 8]
        second = dot_rows(split(hidden), (high, low))
        first = dot_rows(split(latent), pre)
        if g == 0:
            second_sum[...] = second
            first_sum[...] = first
        else:
            second_sum[...] += second
            first_sum[...] += first
    column = lax.broadcasted_iota(jnp.int32, (CH, 256), 1)
    total = jnp.where(((column >> 2) & 1) == 0, second_sum[0:64], second_sum[64:128])
    total = lax.dot_general(
        total, order, (((1,), (0,)), ((), ())), precision=HI, preferred_element_type=F32
    )
    corner = first_sum[0:64, 0:64] + first_sum[64:128, 64:128]
    packed = jnp.concatenate(
        [total, jnp.concatenate([corner[0:32], corner[32:64]], axis=1)], axis=0
    )
    for j in range(8):
        send[j, 96:108, :] = packed[12 * j : 12 * j + 12]


def sum_kernel(*refs):
    parts, latent_out, weights_out = refs
    total = parts[0]
    for j in range(1, 8):
        total = total + parts[j]
    for q in range(24):
        a, t = divmod(q, 4)
        for c in range(4):
            latent_out[c, a : a + 1, 128 * t : 128 * t + 128] = total[4 * q + c : 4 * q + c + 1]
    weights_out[...] = total[96:108]


def pack_kernel(
    press, vel, back_vel, low_x, high_x, low_y, high_y, back_low, back_high, sems
):
    copies = []

    def copy(source, target):
        copies.append(pltpu.make_async_copy(source, target, sems.at[len(copies)]))

    copy(press.at[pl.ds(0, HP)], low_x.at[pl.ds(0, HP)])
    copy(press.at[pl.ds(NXT - HP, HP)], high_x.at[pl.ds(0, HP)])
    copy(press.at[:, pl.ds(0, 8)], low_y.at[:, pl.ds(0, 8)])
    copy(press.at[:, pl.ds(24, 8)], high_y.at[:, pl.ds(0, 8)])
    for place, field in ((0, vel), (1, back_vel)):
        rows = pl.ds(8 + 8 * place, 8)
        copy(field.at[1, :, pl.ds(0, 8)], low_y.at[:, rows])
        copy(field.at[1, :, pl.ds(24, 8)], high_y.at[:, rows])
    copy(vel.at[0, pl.ds(0, HV)], low_x.at[pl.ds(HP, HV)])
    copy(vel.at[0, pl.ds(NXT - HV, HV)], high_x.at[pl.ds(HP, HV)])
    copy(back_vel.at[0, pl.ds(0, HV)], back_low)
    copy(back_vel.at[0, pl.ds(NXT - HV, HV)], back_high)
    for each in copies:
        each.start()
    for each in copies:
        each.wait()


def pack(press, vel, back_vel):
    beside_x, beside_y = shape(HP + HV, NYT, NZ), shape(NXT, 24, NZ)
    back = shape(HV, NYT, NZ)
    return pl.pallas_call(
        pack_kernel,
        out_shape=(beside_x, beside_x, beside_y, beside_y, back, back),
        in_specs=[pl.BlockSpec(memory_space=pltpu.HBM)] * 3,
        out_specs=(VMEM,) * 6,
        scratch_shapes=[pltpu.SemaphoreType.DMA((12,))],
        compiler_params=pltpu.CompilerParams(vmem_limit_bytes=8 * 1024 * 1024),
    )(press, vel, back_vel)


def final_kernel(parts, second_out, first_out):
    whole = jnp.concatenate([parts[j] for j in range(8)], axis=0)
    second_out[...] = whole[:64]
    first_out[0:32] = whole[64:, :64]
    first_out[32:64] = whole[64:, 64:]


def receiver_kernel(pos, observed, after, count_out, obs_out, rows, spread):
    number = pos.shape[1]
    local_x = pos[0:1, :] - lax.axis_index("gx") * NXT
    local_y = pos[1:2, :] - lax.axis_index("gy") * NYT
    inside = (local_x >= 0) & (local_x < NXT) & (local_y >= 0) & (local_y < NYT)
    cell = jnp.where(inside, local_x * NYT + local_y, -1)
    depth_at = pos[2:3, :]
    high = [observed[n : n + 1, :].astype(BF16).astype(F32) for n in range(STEPS)]
    low = [observed[n : n + 1, :] - high[n] for n in range(STEPS)]
    values = [jnp.ones((1, number), F32)] + high + low
    row = lax.broadcasted_iota(jnp.int32, (NYT, number), 0)
    level = lax.broadcasted_iota(jnp.int32, (16, number), 0)

    def fill_rows(x, carry):
        rows[pl.ds(x * NYT, NYT), :] = jnp.where(row == cell - x * NYT, 1.0, 0.0).astype(BF16)
        return carry

    lax.fori_loop(0, NXT, fill_rows, 0)
    for k in range(NZ // 16):
        hit = level + 16 * k == depth_at
        for v, value in enumerate(values):
            spread[NZ * v + 16 * k : NZ * v + 16 * k + 16, :] = jnp.where(hit, value, 0.0).astype(
                BF16
            )

    def multiply(block, carry):
        out = dot(rows[pl.ds(block * 256, 256), :], spread[...], ((1,), (1,)))
        xs = pl.ds(block * 8, 8)
        count_out[xs] = out[:, 0:NZ].reshape(8, NYT, NZ)
        for n in range(STEPS):
            first = out[:, NZ * (1 + n) : NZ * (2 + n)]
            second = out[:, NZ * (4 + n) : NZ * (5 + n)]
            obs_out[n, xs] = (first + second).reshape(8, NYT, NZ)
        return carry

    lax.fori_loop(0, 3, multiply, 0)


def body(
    latent,
    w_first,
    w_second,
    fwd_press,
    fwd_vel,
    adj_press,
    adj_vel,
    src_pos,
    src_amp,
    rec_pos,
    observed,
):
    scalars = (src_pos.reshape(3), src_amp.reshape(3))

    flat = latent.reshape(4, 24, 128).transpose(1, 0, 2).reshape(96, 128)
    blocks = lax.all_to_all(jnp.broadcast_to(flat, (8, 96, 128)), "shot", 0, 0, tiled=True)

    press, back_press = fwd_press[0], adj_press[0]
    vel, back_vel = fwd_vel[0], adj_vel[0]
    edges = pack(press, vel, back_vel)
    beside = exchange(*edges[:4])
    back_edges = list(edges[4:])

    tile = shape(NXT, NYT, NZ)
    beside_x, beside_y = shape(HV, NYT, NZ), shape(NXT, 8, NZ)
    decoded = call(
        decode_kernel,
        [tile, tile, beside_x, beside_x, beside_y, beside_y, tile, tile]
        + [shape(GROUPS, 128, 2 * NZ)] * 2,
        0,
        [w_first, w_second, blocks],
    )
    modulus, buoyancy = decoded[:2]
    material = (buoyancy,) + exchange(*decoded[2:6]) + (modulus,)
    sig_speed, sig_dens, latent_wide, hidden_wide = decoded[6:]

    count, obs = call(
        receiver_kernel,
        [tile, shape(STEPS, NXT, NYT, NZ)],
        0,
        [rec_pos[0], observed[0], decoded[2]],
        [pltpu.VMEM((NXT * NYT, 2048), BF16), pltpu.VMEM((7 * NZ, 2048), BF16)],
        flops=3 * 10**9,
    )
    stored, earlier = [], []
    state_p = (press,) + beside
    state_v = (vel,) + beside
    vz = vel
    offsets = (0, HP, 0, 8)
    for moment in range(STEPS):
        last = moment == STEPS - 1
        vz, dz, slope_z = depth(True, state_p[0], vz, buoyancy)
        extra = [dz] + [back_edges, [count], [count, obs, back_press]][moment]
        outs = step(moment, True, last, offsets, scalars, state_p, state_v, material, extra)
        stored.append(list(outs[:2]) + [slope_z])
        outs = outs[2:]
        if not last:
            earlier.append(outs[0])
            state_v = outs[5:]
        state_p = (outs[0],) + exchange(*outs[1:5])
        if moment == 0:
            back_x = state_p[1:3]
        offsets = (0, 0, 0, 0)
    state_v = (back_vel,) + back_x + beside[2:]
    vz = back_vel
    offsets = (0, HP, 0, 16)
    terms, sums = [], []
    for moment in reversed(range(STEPS)):
        last = moment == 0
        done = depth(False, state_p[0], vz, buoyancy, terms, sums)
        vz, dz, sums = done[0], done[1], list(done[2:])
        if last:
            extra = [dz, vz] + stored[moment] + sums
        else:
            extra = [dz, count, obs, earlier[moment - 1]]
        outs = step(moment, False, last, offsets, (), state_p, state_v, material, extra)
        if last:
            sums = list(outs)
        else:
            state_p = (outs[1],) + exchange(*outs[2:6])
            state_v = outs[6:]
            terms = [outs[0], state_v[0]] + stored[moment]
        offsets = (0, 0, 0, 0)

    (send,) = call(
        grads_kernel,
        [shape(8, 108, 128)],
        0,
        [w_first, w_second] + sums
        + [sig_speed, sig_dens, latent_wide, hidden_wide],
        [pltpu.VMEM((128, 256), F32), pltpu.VMEM((128, 128), F32)],
    )
    parts = lax.all_to_all(send, "shot", 0, 0, tiled=True)
    grad_latent, weights = call(sum_kernel, [shape(4, 6, 512), shape(12, 128)], 0, [parts])
    group = lax.axis_size("gx") * lax.axis_size("gy")
    weights = lax.all_to_all(
        jnp.broadcast_to(weights, (group, 12, 128)), ("gx", "gy"), 0, 0, tiled=True
    )
    weights = jnp.sum(weights, axis=0)
    weights = lax.all_to_all(jnp.broadcast_to(weights, (8, 12, 128)), "shot", 0, 0, tiled=True)
    grad_second, grad_first = call(
        final_kernel, [shape(CH, 128), shape(CH, CH)], 0, [weights]
    )
    return (grad_latent, grad_first, grad_second)


def solution(mesh):
    in_specs = (
        P("shot", "gx", "gy"),
        P(),
        P(),
        P("shot", "gx", "gy", None),
        P("shot", None, "gx", "gy", None),
        P("shot", "gx", "gy", None),
        P("shot", None, "gx", "gy", None),
        P(None, "shot"),
        P(None, "shot"),
        P("shot", None, None),
        P("shot", None, None),
    )
    out_specs = (P("shot", "gx", "gy"), P(), P())
    return jax.shard_map(body, mesh=mesh, in_specs=in_specs, out_specs=out_specs, check_vma=False)
```

```python
import functools

import jax
import jax.numpy as jnp
from jax import lax
from jax.experimental import pallas as pl
from jax.experimental.pallas import tpu as pltpu
from jax.sharding import PartitionSpec as P

CH = 64
STEPS = 3
coeffs = (1225.0 / 1024.0, -245.0 / 3072.0, 49.0 / 5120.0, -5.0 / 7168.0)

NXT, NYT, NZ = 24, 32, 128
GROUPS = 12
HP = 7
HV = 4
HI = lax.Precision.HIGHEST
F32 = jnp.float32
BF16 = jnp.bfloat16
UNROLL = (12, 12, 12)
VMEM = pl.BlockSpec(memory_space=pltpu.VMEM)
SMEM = pl.BlockSpec(memory_space=pltpu.SMEM)


def shape(*dims):
    return jax.ShapeDtypeStruct(dims, F32)


def call(kernel, outs, smem_count, args, scratch=(), flops=10**7):
    nbytes = 4 * sum(a.size for a in args) + 4 * sum(o.size for o in outs)
    return pl.pallas_call(
        kernel,
        out_shape=tuple(outs),
        in_specs=[SMEM] * smem_count + [VMEM] * (len(args) - smem_count),
        out_specs=tuple(VMEM for _ in outs),
        scratch_shapes=list(scratch),
        compiler_params=pltpu.CompilerParams(vmem_limit_bytes=16 * 1024 * 1024),
        cost_estimate=pl.CostEstimate(flops=flops, bytes_accessed=nbytes, transcendentals=0),
    )(*args)


def ring(value, axis, shift):
    count = lax.axis_size(axis)
    return lax.ppermute(value, axis, [(i, (i + shift) % count) for i in range(count)])


def plus(take):
    summed = coeffs[0] * (take(1) - take(0))
    for r in (2, 3, 4):
        summed = summed + coeffs[r - 1] * (take(r) - take(1 - r))
    return summed


def minus(take):
    summed = coeffs[0] * (take(0) - take(-1))
    for r in (2, 3, 4):
        summed = summed + coeffs[r - 1] * (take(r - 1) - take(-r))
    return summed


def step_kernel(moment, forward, last, off_p, off_v, row_p, row_v, *refs):
    refs = list(refs)
    take = refs.pop
    source, amps = (take(0), take(0)) if forward else (None, None)
    press, pxl, pxh, pyl, pyh = [take(0) for _ in range(5)]
    vel, vxl, vxh, vyl, vyh = [take(0) for _ in range(5)]
    buoy, bxl, bxh, byl, byh, modu = [take(0) for _ in range(6)]
    dz = take(0)
    riders = [take(0) for _ in range(4)] if forward and moment == 0 else []
    if forward and moment == 1:
        take(0)
    count = obs = back = earlier = None
    if forward and last:
        count, obs, back = [take(0) for _ in range(3)]
    elif not forward and not last:
        count, obs, earlier = [take(0) for _ in range(3)]
    elif not forward:
        vz_in, div_in, slope_in, slope_z_in, gm_in, gb_in = [take(0) for _ in range(6)]
    if forward:
        div_out, slope_out = take(0), take(0)
    elif last:
        gm_out, gb_out = take(0), take(0)
    else:
        bare_out = take(0)
    ends = forward or not last
    if ends:
        p_out, sxl, sxh, syl, syh = [take(0) for _ in range(5)]
    if not last:
        vel_out, vxl_out, vxh_out, vyl_out, vyh_out = [take(0) for _ in range(5)]
    wide, vx, tall, vy_tall = [take(0) for _ in range(4)]

    at_x, at_y = lax.axis_index("gx"), lax.axis_index("gy")
    low_x = jnp.where(at_x > 0, 1.0, 0.0)
    high_x = jnp.where(at_x < lax.axis_size("gx") - 1, 1.0, 0.0)
    low_y = jnp.where(at_y > 0, 1.0, 0.0)
    high_y = jnp.where(at_y < lax.axis_size("gy") - 1, 1.0, 0.0)
    for i in range(HP):
        wide[i] = pxl[off_p + i] * low_x
        wide[HP + NXT + i] = pxh[off_p + i] * high_x

    nothing = jnp.zeros((8, NZ), F32)

    def copy(x, carry):
        here = press[x]
        wide[x + HP] = here
        tall[x, 0:8] = nothing
        tall[x, 8:16] = pyl[x, row_p : row_p + 8] * low_y
        tall[x, 16:48] = here
        tall[x, 48:56] = pyh[x, row_p : row_p + 8] * high_y
        tall[x, 56:64] = nothing
        vy_tall[x, 0:8] = nothing
        vy_tall[x, 56:64] = nothing
        return carry

    lax.fori_loop(0, NXT, copy, 0, unroll=UNROLL[0])

    def slope_x(i):
        return plus(lambda s: wide[i + 3 + s])

    for i in range(HV):
        vx[i] = low_x * (vxl[off_v + i] - bxl[i] * slope_x(i))
        if not last:
            vxl_out[i] = vx[i]
    for i in range(HV - 1):
        at = HV + NXT + i
        vx[at] = high_x * (vxh[off_v + i] - bxh[i] * slope_x(at))
        if not last:
            vxh_out[i] = vx[at]
    if not last:
        vxh_out[HV - 1] = jnp.zeros((NYT, NZ), F32)

    def first(x, carry):
        b_here = buoy[x]
        slope = slope_x(x + HV)
        new = vel[0, x] - b_here * slope
        vx[x + HV] = new
        slope_y = plus(lambda s: tall[x, 8 + s : 56 + s])
        vy_low = low_y * (vyl[x, row_v : row_v + 8] - byl[x] * slope_y[0:8])
        vy = vel[1, x] - b_here * slope_y[8:40]
        vy_high = high_y * (vyh[x, row_v : row_v + 8] - byh[x] * slope_y[40:48])
        vy_tall[x, 8:16] = vy_low
        vy_tall[x, 16:48] = vy
        vy_tall[x, 48:56] = vy_high
        if not last:
            vel_out[0, x] = new
            vel_out[1, x] = vy
            vyl_out[x] = vy_low
            vyh_out[x] = vy_high
        if forward:
            slope_out[0, x] = slope
            slope_out[1, x] = slope_y[8:40]
        return carry

    lax.fori_loop(0, NXT, first, 0, unroll=UNROLL[1])

    if forward:
        lane = lax.broadcasted_iota(jnp.int32, (NYT, NZ), 1)
        cell = lax.broadcasted_iota(jnp.int32, (NYT, NZ), 0) * NZ + lane
        source_x = source[0] - at_x * NXT
        source_y = source[1] - at_y * NYT
        source_at = jnp.where((source_y >= 0) & (source_y < NYT), source_y * NZ + source[2], -1)
        amplitude = amps[moment]

    def second(x, carry):
        here = press[x]
        diverge = minus(lambda s: vx[x + HV + s])
        diverge = diverge + minus(lambda s: vy_tall[x, 16 + s : 48 + s])
        diverge = diverge + dz[x]
        new = here - modu[x] * diverge
        if forward:
            div_out[x] = diverge
            at = jnp.where(x == source_x, source_at, -1)
            new = new + jnp.where(cell == at, amplitude, 0.0)
            if last:
                new = back[x] + (count[x] * new - obs[moment, x])
        elif last:
            gm_out[x] = gm_in[x] - new * div_in[x]
            gb_out[x] = gb_in[x] - (
                vx[x + HV] * slope_in[0, x]
                + vy_tall[x, 16:48] * slope_in[1, x]
                + vz_in[x] * slope_z_in[x]
            )
        else:
            bare_out[x] = new
            new = new + (count[x] * earlier[x] - obs[moment - 1, x])
        if ends:
            p_out[x] = new
            syl[x, 0:8] = new[0:8]
            syh[x, 0:8] = new[24:32]
            if riders:
                syl[x, 8:16] = riders[2][x]
                syh[x, 8:16] = riders[3][x]
        return carry

    lax.fori_loop(0, NXT, second, 0, unroll=UNROLL[2])
    if ends:
        for i in range(HP):
            sxl[i] = p_out[i]
            sxh[i] = p_out[NXT - HP + i]
        for i in range(HV if riders else 0):
            sxl[HP + i] = riders[0][i]
            sxh[HP + i] = riders[1][i]


def step(moment, forward, last, offsets, scalars, press, vel, material, extra):
    tile = shape(NXT, NYT, NZ)
    two = shape(2, NXT, NYT, NZ)
    beside_y = shape(NXT, 8, NZ)
    outs = [tile, two] if forward else [tile, tile] if last else [tile]
    if forward or not last:
        more = forward and moment == 0
        send_x, send_y = shape(HP + HV * more, NYT, NZ), shape(NXT, 8 + 8 * more, NZ)
        outs += [tile, send_x, send_x, send_y, send_y]
    if not last:
        outs += [two, shape(HV, NYT, NZ), shape(HV, NYT, NZ), beside_y, beside_y]
    args = list(scalars) + list(press) + list(vel) + list(material) + list(extra)
    scratch = [
        pltpu.VMEM(dims, F32)
        for dims in (
            (NXT + 2 * HP, NYT, NZ),
            (NXT + 2 * HV, NYT, NZ),
            (NXT, NYT + 32, NZ),
            (NXT, NYT + 32, NZ),
        )
    ]
    kernel = functools.partial(step_kernel, moment, forward, last, *offsets)
    return call(kernel, outs, len(scalars), args, scratch)


def pieces_of(value):
    high = value.astype(BF16)
    rest = value - high.astype(F32)
    middle = rest.astype(BF16)
    return high, middle, (rest - middle.astype(F32)).astype(BF16)


def band(ahead):
    row = lax.broadcasted_iota(jnp.int32, (NZ, NZ), 0)
    offset = row - lax.broadcasted_iota(jnp.int32, (NZ, NZ), 1) - ahead
    matrix = jnp.zeros((NZ, NZ), F32)
    for r in range(4):
        matrix = jnp.where(offset == r, coeffs[r], matrix)
        matrix = jnp.where(offset == -1 - r, -coeffs[r], matrix)
    high, middle, low = pieces_of(matrix)
    return jnp.concatenate([high, middle, low, high, middle, high], axis=0)


def along_depth(value, right):
    high, middle, low = pieces_of(value.reshape(-1, NZ))
    left = jnp.concatenate([high, high, high, middle, middle, low], axis=1)
    return dot(left, right).reshape(value.shape)


def depth_kernel(slopes, sums, *refs):
    refs = list(refs)
    take = refs.pop
    press, vz_in, buoy = [take(0) for _ in range(3)]
    if sums:
        bare, vel, div_in, slope_in, slope_z_in = [take(0) for _ in range(5)]
        gm_in, gb_in = (take(0), take(0)) if sums == 2 else (None, None)
    vz_out, dz_out = take(0), take(0)
    slope_out = take(0) if slopes else None
    if sums:
        gm_out, gb_out = take(0), take(0)
    right_plus, right_minus = band(1), band(0)

    def layers(block, carry):
        xs = pl.ds(block * 8, 8)
        slope = along_depth(press[xs], right_plus)
        old = vz_in[2, xs] if len(vz_in.shape) == 4 else vz_in[xs]
        vz = old - buoy[xs] * slope
        vz_out[xs] = vz
        dz_out[xs] = along_depth(vz, right_minus)
        if slopes:
            slope_out[xs] = slope
        if sums:
            part_m = -bare[xs] * div_in[xs]
            part_b = vel[0, xs] * slope_in[0, xs] + vel[1, xs] * slope_in[1, xs]
            part_b = -(part_b + old * slope_z_in[xs])
            gm_out[xs] = part_m if gm_in is None else gm_in[xs] + part_m
            gb_out[xs] = part_b if gb_in is None else gb_in[xs] + part_b
        return carry

    lax.fori_loop(0, NXT // 8, layers, 0, unroll=True)


def depth(slopes, press, vz, buoy, terms=(), sums=()):
    tile = shape(NXT, NYT, NZ)
    outs = [tile] * (2 + slopes + (2 if terms else 0))
    mode = 0 if not terms else 2 if sums else 1
    kernel = functools.partial(depth_kernel, slopes, mode)
    return call(kernel, outs, 0, [press, vz, buoy] + list(terms) + list(sums))


def exchange(low_x, high_x, low_y, high_y):
    return (
        ring(high_x, "gx", 1),
        ring(low_x, "gx", -1),
        ring(high_y, "gy", 1),
        ring(low_y, "gy", -1),
    )


def spread_rows():
    row = lax.broadcasted_iota(jnp.int32, (64, 2 * NZ), 0)
    lane = lax.broadcasted_iota(jnp.int32, (64, 2 * NZ), 1)
    same = ((row >> 2) & 1) == (lane >> 7)
    depth = (row >> 3) * 4 + (row & 3)
    return jnp.where(same & (((lane & 127) >> 2) == depth), 1.0, 0.0).astype(BF16)


def split(value):
    high = value.astype(BF16)
    return high, (value - high.astype(F32)).astype(BF16)


def dot(a, b, dims=((1,), (0,))):
    return lax.dot_general(a, b, (dims, ((), ())), preferred_element_type=F32)


def stack_right(value):
    high, low = split(value)
    return jnp.concatenate([high, high, low], axis=0)


def dot_rows(a, b):
    dims = ((1,), (1,))
    return dot(a[0], b[0], dims) + (dot(a[0], b[1], dims) + dot(a[1], b[0], dims))


def reorder():
    row = lax.broadcasted_iota(jnp.int32, (256, 128), 0)
    natural = (((row >> 3) & 7) << 4) + ((row & 3) << 2) + (row >> 6)
    picked = natural == lax.broadcasted_iota(jnp.int32, (256, 128), 1)
    return jnp.where(picked, 1.0, 0.0)


def two_blocks(matrix):
    empty = jnp.zeros((CH, CH), F32)
    return jnp.concatenate(
        [jnp.concatenate([matrix, empty], axis=1), jnp.concatenate([empty, matrix], axis=1)],
        axis=0,
    )


def stack_left(matrix):
    high, low = split(matrix)
    return jnp.concatenate([high, low, high], axis=1)


def phases(dtype):
    lane = lax.broadcasted_iota(jnp.int32, (64, 2 * NZ), 1) & 3
    return [jnp.where(lane == k, 1.0, 0.0).astype(dtype) for k in range(4)]


def decode_kernel(w_first, w_second, blocks, *refs):
    modu, buoy, bxl, bxh, byl, byh, sig_speed, sig_dens, latent_out, hidden_out = refs
    spread = spread_rows()
    spread = jnp.concatenate([spread, spread, spread], axis=0)
    phase = lax.broadcasted_iota(jnp.int32, (64, 2 * NZ), 1) & 3
    mix_first = stack_left(two_blocks(w_first[...]).T)
    chosen = reorder().astype(BF16)
    cell = (lax.broadcasted_iota(jnp.int32, (256, CH), 0) >> 2) & 1
    pieces = []
    for piece in split(w_second[...]):
        rows = dot(chosen, piece, ((1,), (1,)))
        pieces.append(
            jnp.concatenate([jnp.where(cell == b, rows, 0.0) for b in range(2)], axis=1)
        )
    pieces = [piece.astype(BF16) for piece in pieces]
    mix_second = jnp.concatenate([pieces[0], pieces[1], pieces[0]], axis=1)
    for g in range(GROUPS):
        a, half = divmod(g, 2)
        rows = blocks[:, 8 * g : 8 * g + 8, :].reshape(64, 128)
        high, rest = rows.astype(BF16), None
        rest = rows - high.astype(F32)
        middle, low = split(rest)
        pieces = jnp.concatenate([high, middle, low], axis=0)
        latent = dot(pieces, spread, ((0,), (0,)))
        hidden = jnp.tanh(dot(mix_first, stack_right(latent)))
        latent_out[g] = latent
        hidden_out[g] = hidden
        out = dot(mix_second, stack_right(hidden))
        fine = out[0:64]
        for k in (1, 2, 3):
            fine = jnp.where(phase == k, out[64 * k : 64 * k + 64], fine)
        sig = jax.nn.sigmoid(fine)
        s1, s2 = sig[0:32], sig[32:64]
        speed = 0.15 + 0.25 * s1
        dens = 1.0 + 1.5 * s2
        mod = dens * speed * speed
        inv = 1.0 / dens
        for i in range(4):
            for q in range(2):
                x = 4 * a + i
                ys = slice(16 * half + 8 * q, 16 * half + 8 * q + 8)
                part = (slice(8 * i, 8 * i + 8), slice(NZ * q, NZ * q + NZ))
                sig_speed[x, ys] = s1[part]
                sig_dens[x, ys] = s2[part]
                modu[x, ys] = mod[part]
                buoy[x, ys] = inv[part]
    for i in range(HV):
        bxl[i] = buoy[i]
        bxh[i] = buoy[NXT - HV + i]
    byl[...] = buoy[:, 0:8, :]
    byh[...] = buoy[:, 24:32, :]


def grads_kernel(
    w_first, w_second, gm, gb, sig_speed, sig_dens, latent_in, hidden_in, *refs
):
    send, second_sum, first_sum = refs
    spread = spread_rows()
    spread = jnp.concatenate([spread, spread], axis=1)
    masks = phases(BF16)
    back_first = stack_left(two_blocks(w_first[...]))
    order = reorder()
    chosen = order.astype(BF16)
    cell = (lax.broadcasted_iota(jnp.int32, (CH, 256), 1) >> 2) & 1
    pieces = []
    for piece in split(w_second[...]):
        columns = dot(piece, chosen, ((1,), (1,)))
        pieces.append(
            jnp.concatenate([jnp.where(cell == b, columns, 0.0) for b in range(2)], axis=0)
        )
    pieces = [piece.astype(BF16) for piece in pieces]
    back_second = jnp.concatenate([pieces[0], pieces[1], pieces[0]], axis=1)

    def square(field, a, half):
        return jnp.concatenate(
            [
                jnp.concatenate(
                    [field[4 * a + i, 16 * half + 8 * q : 16 * half + 8 * q + 8] for i in range(4)],
                    axis=0,
                )
                for q in range(2)
            ],
            axis=1,
        )

    for g in range(GROUPS):
        a, half = divmod(g, 2)
        s1, s2 = square(sig_speed, a, half), square(sig_dens, a, half)
        g_mod, g_buoy = square(gm, a, half), square(gb, a, half)
        speed = 0.15 + 0.25 * s1
        dens = 1.0 + 1.5 * s2
        grad_speed = g_mod * 2.0 * dens * speed
        grad_dens = g_mod * speed * speed - g_buoy / (dens * dens)
        fine = jnp.concatenate(
            [grad_speed * 0.25 * s1 * (1.0 - s1), grad_dens * 1.5 * s2 * (1.0 - s2)], axis=0
        )
        high, low = split(fine)
        high = jnp.concatenate([high * mask for mask in masks], axis=0)
        low = jnp.concatenate([low * mask for mask in masks], axis=0)
        latent, hidden = latent_in[g], hidden_in[g]
        grad_hidden = dot(back_second, jnp.concatenate([high, high, low], axis=0))
        grad_pre = grad_hidden * (1.0 - hidden * hidden)
        pre = split(grad_pre)
        grad_latent = dot(back_first, jnp.concatenate([pre[0], pre[0], pre[1]], axis=0))
        gathered = dot(
            spread, jnp.concatenate(split(grad_latent), axis=1), ((1,), (1,))
        )
        for j in range(8):
            send[j, 8 * g : 8 * g + 8, :] = gathered[8 * j : 8 * j + 8]
        second = dot_rows(split(hidden), (high, low))
        first = dot_rows(split(latent), pre)
        if g == 0:
            second_sum[...] = second
            first_sum[...] = first
        else:
            second_sum[...] += second
            first_sum[...] += first
    column = lax.broadcasted_iota(jnp.int32, (CH, 256), 1)
    total = jnp.where(((column >> 2) & 1) == 0, second_sum[0:64], second_sum[64:128])
    total = lax.dot_general(
        total, order, (((1,), (0,)), ((), ())), precision=HI, preferred_element_type=F32
    )
    corner = first_sum[0:64, 0:64] + first_sum[64:128, 64:128]
    packed = jnp.concatenate(
        [total, jnp.concatenate([corner[0:32], corner[32:64]], axis=1)], axis=0
    )
    for j in range(8):
        send[j, 96:108, :] = packed[12 * j : 12 * j + 12]


def sum_kernel(*refs):
    parts, latent_out, weights_out = refs
    total = parts[0]
    for j in range(1, 8):
        total = total + parts[j]
    for q in range(24):
        a, t = divmod(q, 4)
        for c in range(4):
            latent_out[c, a : a + 1, 128 * t : 128 * t + 128] = total[4 * q + c : 4 * q + c + 1]
    weights_out[...] = total[96:108]


def pack_kernel(
    press,
    vel,
    back_vel,
    low_x,
    high_x,
    low_y,
    high_y,
    back_low,
    back_high,
    back_low_y,
    back_high_y,
    sems,
):
    copies = []

    def copy(source, target):
        copies.append(pltpu.make_async_copy(source, target, sems.at[len(copies)]))

    copy(press.at[pl.ds(0, HP)], low_x.at[pl.ds(0, HP)])
    copy(press.at[pl.ds(NXT - HP, HP)], high_x.at[pl.ds(0, HP)])
    copy(press.at[:, pl.ds(0, 8)], low_y.at[:, pl.ds(0, 8)])
    copy(press.at[:, pl.ds(24, 8)], high_y.at[:, pl.ds(0, 8)])
    copy(vel.at[1, :, pl.ds(0, 8)], low_y.at[:, pl.ds(8, 8)])
    copy(vel.at[1, :, pl.ds(24, 8)], high_y.at[:, pl.ds(8, 8)])
    copy(back_vel.at[1, :, pl.ds(0, 8)], back_low_y)
    copy(back_vel.at[1, :, pl.ds(24, 8)], back_high_y)
    copy(vel.at[0, pl.ds(0, HV)], low_x.at[pl.ds(HP, HV)])
    copy(vel.at[0, pl.ds(NXT - HV, HV)], high_x.at[pl.ds(HP, HV)])
    copy(back_vel.at[0, pl.ds(0, HV)], back_low)
    copy(back_vel.at[0, pl.ds(NXT - HV, HV)], back_high)
    for each in copies:
        each.start()
    for each in copies:
        each.wait()


def pack(press, vel, back_vel):
    beside_x, beside_y = shape(HP + HV, NYT, NZ), shape(NXT, 16, NZ)
    back, back_y = shape(HV, NYT, NZ), shape(NXT, 8, NZ)
    return pl.pallas_call(
        pack_kernel,
        out_shape=(beside_x, beside_x, beside_y, beside_y, back, back, back_y, back_y),
        in_specs=[pl.BlockSpec(memory_space=pltpu.HBM)] * 3,
        out_specs=(VMEM,) * 8,
        scratch_shapes=[pltpu.SemaphoreType.DMA((12,))],
        compiler_params=pltpu.CompilerParams(vmem_limit_bytes=8 * 1024 * 1024),
    )(press, vel, back_vel)


def final_kernel(parts, second_out, first_out):
    whole = jnp.concatenate([parts[j] for j in range(8)], axis=0)
    second_out[...] = whole[:64]
    first_out[0:32] = whole[64:, :64]
    first_out[32:64] = whole[64:, 64:]


def receiver_kernel(pos, observed, after, count_out, obs_out, rows, spread):
    number = pos.shape[1]
    local_x = pos[0:1, :] - lax.axis_index("gx") * NXT
    local_y = pos[1:2, :] - lax.axis_index("gy") * NYT
    inside = (local_x >= 0) & (local_x < NXT) & (local_y >= 0) & (local_y < NYT)
    cell = jnp.where(inside, local_x * NYT + local_y, -1)
    depth_at = pos[2:3, :]
    high = [observed[n : n + 1, :].astype(BF16).astype(F32) for n in range(STEPS)]
    low = [observed[n : n + 1, :] - high[n] for n in range(STEPS)]
    values = [jnp.ones((1, number), F32)] + high + low
    row = lax.broadcasted_iota(jnp.int32, (NYT, number), 0)
    level = lax.broadcasted_iota(jnp.int32, (16, number), 0)

    def fill_rows(x, carry):
        rows[pl.ds(x * NYT, NYT), :] = jnp.where(row == cell - x * NYT, 1.0, 0.0).astype(BF16)
        return carry

    lax.fori_loop(0, NXT, fill_rows, 0)
    for k in range(NZ // 16):
        hit = level + 16 * k == depth_at
        for v, value in enumerate(values):
            spread[NZ * v + 16 * k : NZ * v + 16 * k + 16, :] = jnp.where(hit, value, 0.0).astype(
                BF16
            )

    def multiply(block, carry):
        out = dot(rows[pl.ds(block * 256, 256), :], spread[...], ((1,), (1,)))
        xs = pl.ds(block * 8, 8)
        count_out[xs] = out[:, 0:NZ].reshape(8, NYT, NZ)
        for n in range(STEPS):
            first = out[:, NZ * (1 + n) : NZ * (2 + n)]
            second = out[:, NZ * (4 + n) : NZ * (5 + n)]
            obs_out[n, xs] = (first + second).reshape(8, NYT, NZ)
        return carry

    lax.fori_loop(0, 3, multiply, 0)


def body(
    latent,
    w_first,
    w_second,
    fwd_press,
    fwd_vel,
    adj_press,
    adj_vel,
    src_pos,
    src_amp,
    rec_pos,
    observed,
):
    scalars = (src_pos.reshape(3), src_amp.reshape(3))

    flat = latent.reshape(4, 24, 128).transpose(1, 0, 2).reshape(96, 128)
    blocks = lax.all_to_all(jnp.broadcast_to(flat, (8, 96, 128)), "shot", 0, 0, tiled=True)

    press, back_press = fwd_press[0], adj_press[0]
    vel, back_vel = fwd_vel[0], adj_vel[0]
    edges = pack(press, vel, back_vel)
    beside = exchange(*edges[:4])
    back_edges = list(edges[4:])

    tile = shape(NXT, NYT, NZ)
    beside_x, beside_y = shape(HV, NYT, NZ), shape(NXT, 8, NZ)
    decoded = call(
        decode_kernel,
        [tile, tile, beside_x, beside_x, beside_y, beside_y, tile, tile]
        + [shape(GROUPS, 128, 2 * NZ)] * 2,
        0,
        [w_first, w_second, blocks],
    )
    modulus, buoyancy = decoded[:2]
    material = (buoyancy,) + exchange(*decoded[2:6]) + (modulus,)
    sig_speed, sig_dens, latent_wide, hidden_wide = decoded[6:]

    count, obs = call(
        receiver_kernel,
        [tile, shape(STEPS, NXT, NYT, NZ)],
        0,
        [rec_pos[0], observed[0], decoded[2]],
        [pltpu.VMEM((NXT * NYT, 2048), BF16), pltpu.VMEM((7 * NZ, 2048), BF16)],
        flops=3 * 10**9,
    )
    stored, earlier = [], []
    state_p = (press,) + beside
    state_v = (vel,) + beside
    vz = vel
    offsets = (0, HP, 0, 8)
    for moment in range(STEPS):
        last = moment == STEPS - 1
        vz, dz, slope_z = depth(True, state_p[0], vz, buoyancy)
        extra = [dz] + [back_edges, [count], [count, obs, back_press]][moment]
        outs = step(moment, True, last, offsets, scalars, state_p, state_v, material, extra)
        stored.append(list(outs[:2]) + [slope_z])
        outs = outs[2:]
        if not last:
            earlier.append(outs[0])
            state_v = outs[5:]
        state_p = (outs[0],) + exchange(*outs[1:5])
        if moment == 0:
            back_beside = state_p[1:]
        offsets = (0, 0, 0, 0)
    state_v = (back_vel,) + back_beside
    vz = back_vel
    offsets = (0, HP, 0, 8)
    terms, sums = [], []
    for moment in reversed(range(STEPS)):
        last = moment == 0
        done = depth(False, state_p[0], vz, buoyancy, terms, sums)
        vz, dz, sums = done[0], done[1], list(done[2:])
        if last:
            extra = [dz, vz] + stored[moment] + sums
        else:
            extra = [dz, count, obs, earlier[moment - 1]]
        outs = step(moment, False, last, offsets, (), state_p, state_v, material, extra)
        if last:
            sums = list(outs)
        else:
            state_p = (outs[1],) + exchange(*outs[2:6])
            state_v = outs[6:]
            terms = [outs[0], state_v[0]] + stored[moment]
        offsets = (0, 0, 0, 0)

    (send,) = call(
        grads_kernel,
        [shape(8, 108, 128)],
        0,
        [w_first, w_second] + sums
        + [sig_speed, sig_dens, latent_wide, hidden_wide],
        [pltpu.VMEM((128, 256), F32), pltpu.VMEM((128, 128), F32)],
    )
    parts = lax.all_to_all(send, "shot", 0, 0, tiled=True)
    grad_latent, weights = call(sum_kernel, [shape(4, 6, 512), shape(12, 128)], 0, [parts])
    group = lax.axis_size("gx") * lax.axis_size("gy")
    weights = lax.all_to_all(
        jnp.broadcast_to(weights, (group, 12, 128)), ("gx", "gy"), 0, 0, tiled=True
    )
    weights = jnp.sum(weights, axis=0)
    weights = lax.all_to_all(jnp.broadcast_to(weights, (8, 12, 128)), "shot", 0, 0, tiled=True)
    grad_second, grad_first = call(
        final_kernel, [shape(CH, 128), shape(CH, CH)], 0, [weights]
    )
    return (grad_latent, grad_first, grad_second)


def solution(mesh):
    in_specs = (
        P("shot", "gx", "gy"),
        P(),
        P(),
        P("shot", "gx", "gy", None),
        P("shot", None, "gx", "gy", None),
        P("shot", "gx", "gy", None),
        P("shot", None, "gx", "gy", None),
        P(None, "shot"),
        P(None, "shot"),
        P("shot", None, None),
        P("shot", None, None),
    )
    out_specs = (P("shot", "gx", "gy"), P(), P())
    return jax.shard_map(body, mesh=mesh, in_specs=in_specs, out_specs=out_specs, check_vma=False)
```

```python
import functools

import jax
import jax.numpy as jnp
from jax import lax
from jax.experimental import pallas as pl
from jax.experimental.pallas import tpu as pltpu
from jax.sharding import PartitionSpec as P

CH = 64
STEPS = 3
coeffs = (1225.0 / 1024.0, -245.0 / 3072.0, 49.0 / 5120.0, -5.0 / 7168.0)

NXT, NYT, NZ = 24, 32, 128
GROUPS = 12
HP = 7
HV = 4
HI = lax.Precision.HIGHEST
F32 = jnp.float32
BF16 = jnp.bfloat16
UNROLL = (12, 12, 12)
VMEM = pl.BlockSpec(memory_space=pltpu.VMEM)
SMEM = pl.BlockSpec(memory_space=pltpu.SMEM)


def shape(*dims):
    return jax.ShapeDtypeStruct(dims, F32)


def call(kernel, outs, smem_count, args, scratch=(), flops=10**7):
    nbytes = 4 * sum(a.size for a in args) + 4 * sum(o.size for o in outs)
    return pl.pallas_call(
        kernel,
        out_shape=tuple(outs),
        in_specs=[SMEM] * smem_count + [VMEM] * (len(args) - smem_count),
        out_specs=tuple(VMEM for _ in outs),
        scratch_shapes=list(scratch),
        compiler_params=pltpu.CompilerParams(vmem_limit_bytes=16 * 1024 * 1024),
        cost_estimate=pl.CostEstimate(flops=flops, bytes_accessed=nbytes, transcendentals=0),
    )(*args)


def ring(value, axis, shift):
    count = lax.axis_size(axis)
    return lax.ppermute(value, axis, [(i, (i + shift) % count) for i in range(count)])


def plus(take):
    summed = coeffs[0] * (take(1) - take(0))
    for r in (2, 3, 4):
        summed = summed + coeffs[r - 1] * (take(r) - take(1 - r))
    return summed


def minus(take):
    summed = coeffs[0] * (take(0) - take(-1))
    for r in (2, 3, 4):
        summed = summed + coeffs[r - 1] * (take(r - 1) - take(-r))
    return summed


def step_kernel(moment, forward, last, off_p, off_v, row_p, row_v, *refs):
    refs = list(refs)
    take = refs.pop
    source, amps = (take(0), take(0)) if forward else (None, None)
    press, pxl, pxh, pyl, pyh = [take(0) for _ in range(5)]
    vel, vxl, vxh, vyl, vyh = [take(0) for _ in range(5)]
    buoy, bxl, bxh, byl, byh, modu = [take(0) for _ in range(6)]
    dz = take(0)
    riders = [take(0) for _ in range(4)] if forward and moment == 0 else []
    if forward and moment == 1:
        take(0)
    count = obs = back = earlier = None
    if forward and last:
        count, obs, back = [take(0) for _ in range(3)]
    elif not forward and not last:
        count, obs, earlier = [take(0) for _ in range(3)]
    elif not forward:
        vz_in, div_in, slope_in, slope_z_in, gm_in, gb_in = [take(0) for _ in range(6)]
    if forward:
        div_out, slope_out = take(0), take(0)
    elif last:
        gm_out, gb_out = take(0), take(0)
    else:
        bare_out = take(0)
    ends = forward or not last
    if ends:
        p_out, sxl, sxh, syl, syh = [take(0) for _ in range(5)]
    if not last:
        vel_out, vxl_out, vxh_out, vyl_out, vyh_out = [take(0) for _ in range(5)]
    wide, vx, tall, vy_tall = [take(0) for _ in range(4)]

    at_x, at_y = lax.axis_index("gx"), lax.axis_index("gy")
    low_x = jnp.where(at_x > 0, 1.0, 0.0)
    high_x = jnp.where(at_x < lax.axis_size("gx") - 1, 1.0, 0.0)
    low_y = jnp.where(at_y > 0, 1.0, 0.0)
    high_y = jnp.where(at_y < lax.axis_size("gy") - 1, 1.0, 0.0)
    for i in range(HP):
        wide[i] = pxl[off_p + i] * low_x
        wide[HP + NXT + i] = pxh[off_p + i] * high_x

    nothing = jnp.zeros((8, NZ), F32)

    def copy(x, carry):
        here = press[x]
        wide[x + HP] = here
        tall[x, 0:8] = nothing
        tall[x, 8:16] = pyl[x, row_p : row_p + 8] * low_y
        tall[x, 16:48] = here
        tall[x, 48:56] = pyh[x, row_p : row_p + 8] * high_y
        tall[x, 56:64] = nothing
        vy_tall[x, 0:8] = nothing
        vy_tall[x, 56:64] = nothing
        return carry

    lax.fori_loop(0, NXT, copy, 0, unroll=UNROLL[0])

    def slope_x(i):
        return plus(lambda s: wide[i + 3 + s])

    for i in range(HV):
        vx[i] = low_x * (vxl[off_v + i] - bxl[i] * slope_x(i))
        if not last:
            vxl_out[i] = vx[i]
    for i in range(HV - 1):
        at = HV + NXT + i
        vx[at] = high_x * (vxh[off_v + i] - bxh[i] * slope_x(at))
        if not last:
            vxh_out[i] = vx[at]
    if not last:
        vxh_out[HV - 1] = jnp.zeros((NYT, NZ), F32)

    def first(x, carry):
        b_here = buoy[x]
        slope = slope_x(x + HV)
        new = vel[0, x] - b_here * slope
        vx[x + HV] = new
        slope_y = plus(lambda s: tall[x, 8 + s : 56 + s])
        vy_low = low_y * (vyl[x, row_v : row_v + 8] - byl[x] * slope_y[0:8])
        vy = vel[1, x] - b_here * slope_y[8:40]
        vy_high = high_y * (vyh[x, row_v : row_v + 8] - byh[x] * slope_y[40:48])
        vy_tall[x, 8:16] = vy_low
        vy_tall[x, 16:48] = vy
        vy_tall[x, 48:56] = vy_high
        if not last:
            vel_out[0, x] = new
            vel_out[1, x] = vy
            vyl_out[x] = vy_low
            vyh_out[x] = vy_high
        if forward:
            slope_out[0, x] = slope
            slope_out[1, x] = slope_y[8:40]
        return carry

    lax.fori_loop(0, NXT, first, 0, unroll=UNROLL[1])

    if forward:
        lane = lax.broadcasted_iota(jnp.int32, (NYT, NZ), 1)
        cell = lax.broadcasted_iota(jnp.int32, (NYT, NZ), 0) * NZ + lane
        source_x = source[0] - at_x * NXT
        source_y = source[1] - at_y * NYT
        source_at = jnp.where((source_y >= 0) & (source_y < NYT), source_y * NZ + source[2], -1)
        amplitude = amps[moment]

    def second(x, carry):
        here = press[x]
        diverge = minus(lambda s: vx[x + HV + s])
        diverge = diverge + minus(lambda s: vy_tall[x, 16 + s : 48 + s])
        diverge = diverge + dz[x]
        new = here - modu[x] * diverge
        if forward:
            div_out[x] = diverge
            at = jnp.where(x == source_x, source_at, -1)
            new = new + jnp.where(cell == at, amplitude, 0.0)
            if last:
                new = back[x] + (count[x] * new - obs[moment, x])
        elif last:
            gm_out[x] = gm_in[x] - new * div_in[x]
            gb_out[x] = gb_in[x] - (
                vx[x + HV] * slope_in[0, x]
                + vy_tall[x, 16:48] * slope_in[1, x]
                + vz_in[x] * slope_z_in[x]
            )
        else:
            bare_out[x] = new
            new = new + (count[x] * earlier[x] - obs[moment - 1, x])
        if ends:
            p_out[x] = new
            syl[x, 0:8] = new[0:8]
            syh[x, 0:8] = new[24:32]
            if riders:
                syl[x, 8:16] = riders[2][x]
                syh[x, 8:16] = riders[3][x]
        return carry

    lax.fori_loop(0, NXT, second, 0, unroll=UNROLL[2])
    if ends:
        for i in range(HP):
            sxl[i] = p_out[i]
            sxh[i] = p_out[NXT - HP + i]
        for i in range(HV if riders else 0):
            sxl[HP + i] = riders[0][i]
            sxh[HP + i] = riders[1][i]


def step(moment, forward, last, offsets, scalars, press, vel, material, extra):
    tile = shape(NXT, NYT, NZ)
    two = shape(2, NXT, NYT, NZ)
    beside_y = shape(NXT, 8, NZ)
    outs = [tile, two] if forward else [tile, tile] if last else [tile]
    if forward or not last:
        more = forward and moment == 0
        send_x, send_y = shape(HP + HV * more, NYT, NZ), shape(NXT, 8 + 8 * more, NZ)
        outs += [tile, send_x, send_x, send_y, send_y]
    if not last:
        outs += [two, shape(HV, NYT, NZ), shape(HV, NYT, NZ), beside_y, beside_y]
    args = list(scalars) + list(press) + list(vel) + list(material) + list(extra)
    scratch = [
        pltpu.VMEM(dims, F32)
        for dims in (
            (NXT + 2 * HP, NYT, NZ),
            (NXT + 2 * HV, NYT, NZ),
            (NXT, NYT + 32, NZ),
            (NXT, NYT + 32, NZ),
        )
    ]
    kernel = functools.partial(step_kernel, moment, forward, last, *offsets)
    return call(kernel, outs, len(scalars), args, scratch)


def pieces_of(value):
    high = value.astype(BF16)
    rest = value - high.astype(F32)
    middle = rest.astype(BF16)
    return high, middle, (rest - middle.astype(F32)).astype(BF16)


def band(ahead):
    row = lax.broadcasted_iota(jnp.int32, (NZ, NZ), 0)
    offset = row - lax.broadcasted_iota(jnp.int32, (NZ, NZ), 1) - ahead
    matrix = jnp.zeros((NZ, NZ), F32)
    for r in range(4):
        matrix = jnp.where(offset == r, coeffs[r], matrix)
        matrix = jnp.where(offset == -1 - r, -coeffs[r], matrix)
    high, middle, low = pieces_of(matrix)
    return jnp.concatenate([high, middle, low, high, middle, high], axis=0)


def along_depth(value, right):
    high, middle, low = pieces_of(value.reshape(-1, NZ))
    left = jnp.concatenate([high, high, high, middle, middle, low], axis=1)
    return dot(left, right).reshape(value.shape)


def depth_kernel(slopes, sums, *refs):
    refs = list(refs)
    take = refs.pop
    press, vz_in, buoy = [take(0) for _ in range(3)]
    if sums:
        bare, vel, div_in, slope_in, slope_z_in = [take(0) for _ in range(5)]
        gm_in, gb_in = (take(0), take(0)) if sums == 2 else (None, None)
    vz_out, dz_out = take(0), take(0)
    slope_out = take(0) if slopes else None
    if sums:
        gm_out, gb_out = take(0), take(0)
    right_plus, right_minus = band(1), band(0)

    def layers(block, carry):
        xs = pl.ds(block * 8, 8)
        slope = along_depth(press[xs], right_plus)
        old = vz_in[2, xs] if len(vz_in.shape) == 4 else vz_in[xs]
        vz = old - buoy[xs] * slope
        vz_out[xs] = vz
        dz_out[xs] = along_depth(vz, right_minus)
        if slopes:
            slope_out[xs] = slope
        if sums:
            part_m = -bare[xs] * div_in[xs]
            part_b = vel[0, xs] * slope_in[0, xs] + vel[1, xs] * slope_in[1, xs]
            part_b = -(part_b + old * slope_z_in[xs])
            gm_out[xs] = part_m if gm_in is None else gm_in[xs] + part_m
            gb_out[xs] = part_b if gb_in is None else gb_in[xs] + part_b
        return carry

    lax.fori_loop(0, NXT // 8, layers, 0, unroll=True)


def depth(slopes, press, vz, buoy, terms=(), sums=()):
    tile = shape(NXT, NYT, NZ)
    outs = [tile] * (2 + slopes + (2 if terms else 0))
    mode = 0 if not terms else 2 if sums else 1
    kernel = functools.partial(depth_kernel, slopes, mode)
    return call(kernel, outs, 0, [press, vz, buoy] + list(terms) + list(sums))


def exchange(low_x, high_x, low_y, high_y):
    return (
        ring(high_x, "gx", 1),
        ring(low_x, "gx", -1),
        ring(high_y, "gy", 1),
        ring(low_y, "gy", -1),
    )


def spread_rows():
    row = lax.broadcasted_iota(jnp.int32, (64, 2 * NZ), 0)
    lane = lax.broadcasted_iota(jnp.int32, (64, 2 * NZ), 1)
    same = ((row >> 2) & 1) == (lane >> 7)
    depth = (row >> 3) * 4 + (row & 3)
    return jnp.where(same & (((lane & 127) >> 2) == depth), 1.0, 0.0).astype(BF16)


def split(value):
    high = value.astype(BF16)
    return high, (value - high.astype(F32)).astype(BF16)


def dot(a, b, dims=((1,), (0,))):
    return lax.dot_general(a, b, (dims, ((), ())), preferred_element_type=F32)


def stack_right(value):
    high, low = split(value)
    return jnp.concatenate([high, high, low], axis=0)


def dot_rows(a, b):
    dims = ((1,), (1,))
    return dot(a[0], b[0], dims) + (dot(a[0], b[1], dims) + dot(a[1], b[0], dims))


def reorder():
    row = lax.broadcasted_iota(jnp.int32, (256, 128), 0)
    natural = (((row >> 3) & 7) << 4) + ((row & 3) << 2) + (row >> 6)
    picked = natural == lax.broadcasted_iota(jnp.int32, (256, 128), 1)
    return jnp.where(picked, 1.0, 0.0)


def two_blocks(matrix):
    empty = jnp.zeros((CH, CH), F32)
    return jnp.concatenate(
        [jnp.concatenate([matrix, empty], axis=1), jnp.concatenate([empty, matrix], axis=1)],
        axis=0,
    )


def stack_left(matrix):
    high, low = split(matrix)
    return jnp.concatenate([high, low, high], axis=1)


def phases(dtype):
    lane = lax.broadcasted_iota(jnp.int32, (64, 2 * NZ), 1) & 3
    return [jnp.where(lane == k, 1.0, 0.0).astype(dtype) for k in range(4)]


def decode_kernel(w_first, w_second, blocks, vel_low, vel_high, *refs):
    modu, buoy, bxl, bxh, byl, byh, sig_speed, sig_dens, latent_out, hidden_out = refs
    spread = spread_rows()
    spread = jnp.concatenate([spread, spread, spread], axis=0)
    phase = lax.broadcasted_iota(jnp.int32, (64, 2 * NZ), 1) & 3
    mix_first = stack_left(two_blocks(w_first[...]).T)
    chosen = reorder().astype(BF16)
    cell = (lax.broadcasted_iota(jnp.int32, (256, CH), 0) >> 2) & 1
    pieces = []
    for piece in split(w_second[...]):
        rows = dot(chosen, piece, ((1,), (1,)))
        pieces.append(
            jnp.concatenate([jnp.where(cell == b, rows, 0.0) for b in range(2)], axis=1)
        )
    pieces = [piece.astype(BF16) for piece in pieces]
    mix_second = jnp.concatenate([pieces[0], pieces[1], pieces[0]], axis=1)
    for g in range(GROUPS):
        a, half = divmod(g, 2)
        rows = blocks[:, 8 * g : 8 * g + 8, :].reshape(64, 128)
        high, rest = rows.astype(BF16), None
        rest = rows - high.astype(F32)
        middle, low = split(rest)
        pieces = jnp.concatenate([high, middle, low], axis=0)
        latent = dot(pieces, spread, ((0,), (0,)))
        hidden = jnp.tanh(dot(mix_first, stack_right(latent)))
        latent_out[g] = latent
        hidden_out[g] = hidden
        out = dot(mix_second, stack_right(hidden))
        fine = out[0:64]
        for k in (1, 2, 3):
            fine = jnp.where(phase == k, out[64 * k : 64 * k + 64], fine)
        sig = jax.nn.sigmoid(fine)
        s1, s2 = sig[0:32], sig[32:64]
        speed = 0.15 + 0.25 * s1
        dens = 1.0 + 1.5 * s2
        mod = dens * speed * speed
        inv = 1.0 / dens
        for i in range(4):
            for q in range(2):
                x = 4 * a + i
                ys = slice(16 * half + 8 * q, 16 * half + 8 * q + 8)
                part = (slice(8 * i, 8 * i + 8), slice(NZ * q, NZ * q + NZ))
                sig_speed[x, ys] = s1[part]
                sig_dens[x, ys] = s2[part]
                modu[x, ys] = mod[part]
                buoy[x, ys] = inv[part]
    for i in range(HV):
        bxl[i] = buoy[i]
        bxh[i] = buoy[NXT - HV + i]
        bxl[HV + i] = vel_low[i]
        bxh[HV + i] = vel_high[i]
    byl[...] = buoy[:, 0:8, :]
    byh[...] = buoy[:, 24:32, :]


def grads_kernel(
    w_first, w_second, gm, gb, sig_speed, sig_dens, latent_in, hidden_in, *refs
):
    send, second_sum, first_sum = refs
    spread = spread_rows()
    spread = jnp.concatenate([spread, spread], axis=1)
    masks = phases(BF16)
    back_first = stack_left(two_blocks(w_first[...]))
    order = reorder()
    chosen = order.astype(BF16)
    cell = (lax.broadcasted_iota(jnp.int32, (CH, 256), 1) >> 2) & 1
    pieces = []
    for piece in split(w_second[...]):
        columns = dot(piece, chosen, ((1,), (1,)))
        pieces.append(
            jnp.concatenate([jnp.where(cell == b, columns, 0.0) for b in range(2)], axis=0)
        )
    pieces = [piece.astype(BF16) for piece in pieces]
    back_second = jnp.concatenate([pieces[0], pieces[1], pieces[0]], axis=1)

    def square(field, a, half):
        return jnp.concatenate(
            [
                jnp.concatenate(
                    [field[4 * a + i, 16 * half + 8 * q : 16 * half + 8 * q + 8] for i in range(4)],
                    axis=0,
                )
                for q in range(2)
            ],
            axis=1,
        )

    for g in range(GROUPS):
        a, half = divmod(g, 2)
        s1, s2 = square(sig_speed, a, half), square(sig_dens, a, half)
        g_mod, g_buoy = square(gm, a, half), square(gb, a, half)
        speed = 0.15 + 0.25 * s1
        dens = 1.0 + 1.5 * s2
        grad_speed = g_mod * 2.0 * dens * speed
        grad_dens = g_mod * speed * speed - g_buoy / (dens * dens)
        fine = jnp.concatenate(
            [grad_speed * 0.25 * s1 * (1.0 - s1), grad_dens * 1.5 * s2 * (1.0 - s2)], axis=0
        )
        high, low = split(fine)
        high = jnp.concatenate([high * mask for mask in masks], axis=0)
        low = jnp.concatenate([low * mask for mask in masks], axis=0)
        latent, hidden = latent_in[g], hidden_in[g]
        grad_hidden = dot(back_second, jnp.concatenate([high, high, low], axis=0))
        grad_pre = grad_hidden * (1.0 - hidden * hidden)
        pre = split(grad_pre)
        grad_latent = dot(back_first, jnp.concatenate([pre[0], pre[0], pre[1]], axis=0))
        gathered = dot(
            spread, jnp.concatenate(split(grad_latent), axis=1), ((1,), (1,))
        )
        for j in range(8):
            send[j, 8 * g : 8 * g + 8, :] = gathered[8 * j : 8 * j + 8]
        second = dot_rows(split(hidden), (high, low))
        first = dot_rows(split(latent), pre)
        if g == 0:
            second_sum[...] = second
            first_sum[...] = first
        else:
            second_sum[...] += second
            first_sum[...] += first
    column = lax.broadcasted_iota(jnp.int32, (CH, 256), 1)
    total = jnp.where(((column >> 2) & 1) == 0, second_sum[0:64], second_sum[64:128])
    total = lax.dot_general(
        total, order, (((1,), (0,)), ((), ())), precision=HI, preferred_element_type=F32
    )
    corner = first_sum[0:64, 0:64] + first_sum[64:128, 64:128]
    packed = jnp.concatenate(
        [total, jnp.concatenate([corner[0:32], corner[32:64]], axis=1)], axis=0
    )
    for j in range(8):
        send[j, 96:108, :] = packed[12 * j : 12 * j + 12]


def sum_kernel(*refs):
    parts, latent_out, weights_out = refs
    total = parts[0]
    for j in range(1, 8):
        total = total + parts[j]
    for q in range(24):
        a, t = divmod(q, 4)
        for c in range(4):
            latent_out[c, a : a + 1, 128 * t : 128 * t + 128] = total[4 * q + c : 4 * q + c + 1]
    weights_out[...] = total[96:108]


def pack_kernel(
    press,
    vel,
    back_vel,
    low_x,
    high_x,
    low_y,
    high_y,
    back_low,
    back_high,
    back_low_y,
    back_high_y,
    vel_low,
    vel_high,
    sems,
):
    copies = []

    def copy(source, target):
        copies.append(pltpu.make_async_copy(source, target, sems.at[len(copies)]))

    copy(press.at[pl.ds(0, HP)], low_x.at[pl.ds(0, HP)])
    copy(press.at[pl.ds(NXT - HP, HP)], high_x.at[pl.ds(0, HP)])
    copy(press.at[:, pl.ds(0, 8)], low_y.at[:, pl.ds(0, 8)])
    copy(press.at[:, pl.ds(24, 8)], high_y.at[:, pl.ds(0, 8)])
    copy(vel.at[1, :, pl.ds(0, 8)], low_y.at[:, pl.ds(8, 8)])
    copy(vel.at[1, :, pl.ds(24, 8)], high_y.at[:, pl.ds(8, 8)])
    copy(back_vel.at[1, :, pl.ds(0, 8)], back_low_y)
    copy(back_vel.at[1, :, pl.ds(24, 8)], back_high_y)
    copy(vel.at[0, pl.ds(0, HV)], vel_low)
    copy(vel.at[0, pl.ds(NXT - HV, HV)], vel_high)
    copy(back_vel.at[0, pl.ds(0, HV)], back_low)
    copy(back_vel.at[0, pl.ds(NXT - HV, HV)], back_high)
    for each in copies:
        each.start()
    for each in copies:
        each.wait()


def pack(press, vel, back_vel):
    beside_x, beside_y = shape(HP, NYT, NZ), shape(NXT, 16, NZ)
    back, back_y = shape(HV, NYT, NZ), shape(NXT, 8, NZ)
    return pl.pallas_call(
        pack_kernel,
        out_shape=(beside_x, beside_x, beside_y, beside_y, back, back, back_y, back_y, back, back),
        in_specs=[pl.BlockSpec(memory_space=pltpu.HBM)] * 3,
        out_specs=(VMEM,) * 10,
        scratch_shapes=[pltpu.SemaphoreType.DMA((12,))],
        compiler_params=pltpu.CompilerParams(vmem_limit_bytes=8 * 1024 * 1024),
    )(press, vel, back_vel)


def final_kernel(parts, second_out, first_out):
    whole = jnp.concatenate([parts[j] for j in range(8)], axis=0)
    second_out[...] = whole[:64]
    first_out[0:32] = whole[64:, :64]
    first_out[32:64] = whole[64:, 64:]


def receiver_kernel(pos, observed, after, count_out, obs_out, rows, spread):
    number = pos.shape[1]
    local_x = pos[0:1, :] - lax.axis_index("gx") * NXT
    local_y = pos[1:2, :] - lax.axis_index("gy") * NYT
    inside = (local_x >= 0) & (local_x < NXT) & (local_y >= 0) & (local_y < NYT)
    cell = jnp.where(inside, local_x * NYT + local_y, -1)
    depth_at = pos[2:3, :]
    high = [observed[n : n + 1, :].astype(BF16).astype(F32) for n in range(STEPS)]
    low = [observed[n : n + 1, :] - high[n] for n in range(STEPS)]
    values = [jnp.ones((1, number), F32)] + high + low
    row = lax.broadcasted_iota(jnp.int32, (NYT, number), 0)
    level = lax.broadcasted_iota(jnp.int32, (16, number), 0)

    def fill_rows(x, carry):
        rows[pl.ds(x * NYT, NYT), :] = jnp.where(row == cell - x * NYT, 1.0, 0.0).astype(BF16)
        return carry

    lax.fori_loop(0, NXT, fill_rows, 0)
    for k in range(NZ // 16):
        hit = level + 16 * k == depth_at
        for v, value in enumerate(values):
            spread[NZ * v + 16 * k : NZ * v + 16 * k + 16, :] = jnp.where(hit, value, 0.0).astype(
                BF16
            )

    def multiply(block, carry):
        out = dot(rows[pl.ds(block * 256, 256), :], spread[...], ((1,), (1,)))
        xs = pl.ds(block * 8, 8)
        count_out[xs] = out[:, 0:NZ].reshape(8, NYT, NZ)
        for n in range(STEPS):
            first = out[:, NZ * (1 + n) : NZ * (2 + n)]
            second = out[:, NZ * (4 + n) : NZ * (5 + n)]
            obs_out[n, xs] = (first + second).reshape(8, NYT, NZ)
        return carry

    lax.fori_loop(0, 3, multiply, 0)


def body(
    latent,
    w_first,
    w_second,
    fwd_press,
    fwd_vel,
    adj_press,
    adj_vel,
    src_pos,
    src_amp,
    rec_pos,
    observed,
):
    scalars = (src_pos.reshape(3), src_amp.reshape(3))

    flat = latent.reshape(4, 24, 128).transpose(1, 0, 2).reshape(96, 128)
    blocks = lax.all_to_all(jnp.broadcast_to(flat, (8, 96, 128)), "shot", 0, 0, tiled=True)

    press, back_press = fwd_press[0], adj_press[0]
    vel, back_vel = fwd_vel[0], adj_vel[0]
    edges = pack(press, vel, back_vel)
    beside = exchange(*edges[:4])
    back_edges = list(edges[4:8])

    tile = shape(NXT, NYT, NZ)
    beside_x, beside_y = shape(2 * HV, NYT, NZ), shape(NXT, 8, NZ)
    decoded = call(
        decode_kernel,
        [tile, tile, beside_x, beside_x, beside_y, beside_y, tile, tile]
        + [shape(GROUPS, 128, 2 * NZ)] * 2,
        0,
        [w_first, w_second, blocks, edges[8], edges[9]],
    )
    modulus, buoyancy = decoded[:2]
    sides = exchange(*decoded[2:6])
    material = (buoyancy,) + sides + (modulus,)
    sig_speed, sig_dens, latent_wide, hidden_wide = decoded[6:]

    count, obs = call(
        receiver_kernel,
        [tile, shape(STEPS, NXT, NYT, NZ)],
        0,
        [rec_pos[0], observed[0], decoded[2]],
        [pltpu.VMEM((NXT * NYT, 2048), BF16), pltpu.VMEM((7 * NZ, 2048), BF16)],
        flops=3 * 10**9,
    )
    stored, earlier = [], []
    state_p = (press,) + beside
    state_v = (vel,) + sides[:2] + beside[2:]
    vz = vel
    offsets = (0, HV, 0, 8)
    for moment in range(STEPS):
        last = moment == STEPS - 1
        vz, dz, slope_z = depth(True, state_p[0], vz, buoyancy)
        extra = [dz] + [back_edges, [count], [count, obs, back_press]][moment]
        outs = step(moment, True, last, offsets, scalars, state_p, state_v, material, extra)
        stored.append(list(outs[:2]) + [slope_z])
        outs = outs[2:]
        if not last:
            earlier.append(outs[0])
            state_v = outs[5:]
        state_p = (outs[0],) + exchange(*outs[1:5])
        if moment == 0:
            back_beside = state_p[1:]
        offsets = (0, 0, 0, 0)
    state_v = (back_vel,) + back_beside
    vz = back_vel
    offsets = (0, HP, 0, 8)
    terms, sums = [], []
    for moment in reversed(range(STEPS)):
        last = moment == 0
        done = depth(False, state_p[0], vz, buoyancy, terms, sums)
        vz, dz, sums = done[0], done[1], list(done[2:])
        if last:
            extra = [dz, vz] + stored[moment] + sums
        else:
            extra = [dz, count, obs, earlier[moment - 1]]
        outs = step(moment, False, last, offsets, (), state_p, state_v, material, extra)
        if last:
            sums = list(outs)
        else:
            state_p = (outs[1],) + exchange(*outs[2:6])
            state_v = outs[6:]
            terms = [outs[0], state_v[0]] + stored[moment]
        offsets = (0, 0, 0, 0)

    (send,) = call(
        grads_kernel,
        [shape(8, 108, 128)],
        0,
        [w_first, w_second] + sums
        + [sig_speed, sig_dens, latent_wide, hidden_wide],
        [pltpu.VMEM((128, 256), F32), pltpu.VMEM((128, 128), F32)],
    )
    parts = lax.all_to_all(send, "shot", 0, 0, tiled=True)
    grad_latent, weights = call(sum_kernel, [shape(4, 6, 512), shape(12, 128)], 0, [parts])
    group = lax.axis_size("gx") * lax.axis_size("gy")
    weights = lax.all_to_all(
        jnp.broadcast_to(weights, (group, 12, 128)), ("gx", "gy"), 0, 0, tiled=True
    )
    weights = jnp.sum(weights, axis=0)
    weights = lax.all_to_all(jnp.broadcast_to(weights, (8, 12, 128)), "shot", 0, 0, tiled=True)
    grad_second, grad_first = call(
        final_kernel, [shape(CH, 128), shape(CH, CH)], 0, [weights]
    )
    return (grad_latent, grad_first, grad_second)


def solution(mesh):
    in_specs = (
        P("shot", "gx", "gy"),
        P(),
        P(),
        P("shot", "gx", "gy", None),
        P("shot", None, "gx", "gy", None),
        P("shot", "gx", "gy", None),
        P("shot", None, "gx", "gy", None),
        P(None, "shot"),
        P(None, "shot"),
        P("shot", None, None),
        P("shot", None, None),
    )
    out_specs = (P("shot", "gx", "gy"), P(), P())
    return jax.shard_map(body, mesh=mesh, in_specs=in_specs, out_specs=out_specs, check_vma=False)
```
